128 devices in a mesh: seq: 32 (over y, x, z_lo), chan: 4 (over z_hi, core).
Axes of the slice: x: 4, y: 4, z: 4 (z_hi: 2, z_lo: 2; z = z_hi * 2 + z_lo), core: 2. Of those that a mesh axis runs over, the one named last changes fastest.
Arguments:
- query_act: bfloat16 [4096, 4096], P('seq', 'chan'), may hold values from -6 to 6
- key_act: bfloat16 [4096, 4096], P('seq', 'chan'), may hold values from -6 to 6
- value_act: bfloat16 [4096, 4096], P('seq', 'chan'), may hold values from -6 to 6
- residue: float32 [16, 4096], P(None, 'chan'), may hold values from -2 to 2
- decay_rate: float32 [16, 4096], P(None, 'chan'), may hold values from 0.00012207031 to 0.03
- out_weight: bfloat16 [8192, 4096], P(None, 'chan'), may hold values from -0.0625 to 0.0625
- grad_out: bfloat16 [4096, 8192], P('seq', 'chan'), may hold values from -12 to 12
Outputs:
- grad_query: bfloat16 [4096, 4096], P('seq', 'chan')
- grad_key: bfloat16 [4096, 4096], P('seq', 'chan')
- grad_value: bfloat16 [4096, 4096], P('seq', 'chan')
- grad_out_weight: float32 [8192, 4096], P('seq', 'chan')
- grad_residue: float32 [16, 4096], P(None, 'chan')
- grad_log_rate: float32 [16, 4096], P(None, 'chan')
The draws below stay inside these ranges and needn't reach their ends.
All inputs are finite; a program needn't handle non-finite values.
Results may differ from the reference program's by a relative error of at most 0.015.
Values may be sent and summed in bfloat16 or wider, within the bound.
A program may use at most 192 MiB of HBM per device.

```python
import math
import jax
import jax.numpy as jnp
from jax import lax

CH = 4096
DMODEL = 8192
MODES = 16
TOKENS = 4096


def strengthened(array, own_key, source, target, parts, factor):
    owner, partner = [(jnp.arange(array.shape[dim]) // (array.shape[dim] // parts)).reshape([-1 if axis == dim else 1 for axis in range(array.ndim)]) for dim in (source, target)]
    chosen = jax.random.permutation(own_key, parts)[partner]
    strong = (owner == chosen) | (owner == (partner + parts // 2) % parts)
    return jnp.where(strong, factor * array, array)


def block_scale(own_key, extent, shards, least, largest):
    factor_of, own = 1.0, jax.random.fold_in(own_key, 6)
    for axis_at, shards_of in shards:
        draws = jnp.exp(jax.random.uniform(jax.random.fold_in(own, axis_at), (shards_of,), jnp.float32, least / len(shards), largest / len(shards)))
        factor_of = factor_of * jnp.repeat(draws, extent[axis_at] // shards_of).reshape([-1 if axis == axis_at else 1 for axis in range(len(extent))])
    return factor_of


def normal_values(own_key, extent, scale, bound, pieces=(), held_as=jnp.bfloat16):
    gain = block_scale(own_key, extent, pieces, -0.22, 0.18) if pieces else 1.0
    result = jax.random.normal(own_key, extent, jnp.float32) * scale * gain
    return jnp.minimum(jnp.maximum(result, -bound), bound).astype(held_as)


def bell_draw_with(key, dims, deviation, bound, cuts, heavy, kind=jnp.bfloat16):
    values = deviation * jax.random.normal(key, dims, jnp.float32)
    if cuts:
        values = values * block_scale(key, dims, cuts, -0.22, 0.18)
    return jnp.clip(strengthened(values, jax.random.fold_in(key, 3), *heavy), -bound, bound).astype(kind)


def setup_inputs(seed: int = 0) -> dict:
    key_of = jax.random.split(jax.random.key(seed), 8)
    query_act = normal_values(key_of[0], (TOKENS, CH), 1.0, 6.0, ((0, 32), (1, 4)))
    key_act = normal_values(key_of[1], (TOKENS, CH), 1.0, 6.0, ((0, 32), (1, 4)))
    value_act = normal_values(key_of[2], (TOKENS, CH), 1.0, 6.0, ((0, 32), (1, 4)))
    residue = normal_values(key_of[3], (MODES, CH), 0.35, 2.0, ((1, 4),), jnp.float32)
    decay_rate = jnp.clip(jnp.exp(math.log(0.03) - 5.5043554 * jax.random.uniform(key_of[4], (MODES, CH), jnp.float32) ** block_scale(key_of[4], (MODES, CH), ((1, 4),), -0.2, 0.2)), 0.00012207031, 0.03)
    out_weight = normal_values(key_of[5], (DMODEL, CH), DMODEL ** -0.5, 0.0625, ((1, 4),))
    grad_out = bell_draw_with(key_of[6], (TOKENS, DMODEL), 1.0, 12.0, ((0, 32), (1, 4)), (0, 1, 32, 2.75))
    return {"query_act": query_act, "key_act": key_act, "value_act": value_act, "residue": residue, "decay_rate": decay_rate, "out_weight": out_weight, "grad_out": grad_out}


def reference(query_act, key_act, value_act, residue, decay_rate, out_weight, grad_out):
    length = query_act.shape[0]
    padded = 2 * length
    grad_scale = float(TOKENS) ** (-0.5)
    places = jnp.arange(length).astype(jnp.float32)[:, None]

    def add_mode(kernel, mode_pair):
        mode_res, mode_rate = mode_pair
        term = mode_res[None, :] * jnp.sqrt(mode_rate)[None, :] * jnp.exp(-mode_rate[None, :] * places)
        return (kernel + term, None)
    kernel, _ = lax.scan(add_mode, jnp.zeros(query_act.shape, jnp.float32), (residue, decay_rate))

    def spectrum(signal):
        return jnp.fft.rfft(signal.astype(jnp.float32), n=padded, axis=0)

    def restore(spec_values):
        return jnp.fft.irfft(spec_values, n=padded, axis=0)[:length]
    conv_input = (key_act.astype(jnp.float32) * value_act.astype(jnp.float32)).astype(jnp.bfloat16)
    input_spec = spectrum(conv_input)
    kernel_spec = spectrum(kernel)
    conv_out = restore(kernel_spec * input_spec).astype(jnp.bfloat16)
    gated_act = (query_act.astype(jnp.float32) * conv_out.astype(jnp.float32)).astype(jnp.bfloat16)
    grad_mixed = jnp.dot(grad_out, out_weight, preferred_element_type=jnp.float32).astype(jnp.bfloat16)
    grad_weight = jnp.dot(grad_out.T, gated_act, preferred_element_type=jnp.float32) * grad_scale
    grad_query = (grad_mixed.astype(jnp.float32) * conv_out.astype(jnp.float32)).astype(jnp.bfloat16)
    conv_cot = (grad_mixed.astype(jnp.float32) * query_act.astype(jnp.float32)).astype(jnp.bfloat16)
    cot_spec = spectrum(conv_cot)
    grad_conv = restore(jnp.conj(kernel_spec) * cot_spec).astype(jnp.bfloat16)
    filter_values = restore(jnp.conj(input_spec) * cot_spec)
    grad_key = (grad_conv.astype(jnp.float32) * value_act.astype(jnp.float32)).astype(jnp.bfloat16)
    grad_value = (grad_conv.astype(jnp.float32) * key_act.astype(jnp.float32)).astype(jnp.bfloat16)

    def mode_grads(mode_pair):
        mode_res, mode_rate = mode_pair
        mode_basis = jnp.sqrt(mode_rate)[None, :] * jnp.exp(-mode_rate[None, :] * places)
        weighted = filter_values * mode_basis
        plain_sum = lax.optimization_barrier(jnp.sum(weighted, axis=0))
        ramp_sum = lax.optimization_barrier(jnp.sum(weighted * (0.5 - mode_rate[None, :] * places), axis=0))
        return (plain_sum * grad_scale, mode_res * ramp_sum * grad_scale)
    grad_res, grad_log = lax.map(mode_grads, (residue, decay_rate))
    return (grad_query, grad_key, grad_value, grad_weight, grad_res, grad_log)
```

```python
import jax
import jax.numpy as jnp
from jax import lax
from jax.experimental import pallas as pl
from jax.experimental.pallas import tpu as pltpu
from jax.sharding import PartitionSpec as P

MESH = pl.DeviceIdType.MESH
F32 = jnp.float32
BF16 = jnp.bfloat16
ROWS = 128
COLS = 1024
TILES = 8
MODES = 16
PLANE = 8
LAYERS = 4
PARTS = 4
DPART = 2048
PIECE = 256
CHUNKS = 4
WIDE = COLS // CHUNKS
DEPTH = 512


def rows8(index):
    return pl.ds(pl.multiple_of(index * 8, 8), 8)


def body(
    q_ref, k_ref, v_ref, g_ref, res_ref, rate_ref, w_ref,
    gq_ref, gk_ref, gv_ref, gw_ref, gr_ref, gl_ref,
    wv, xs, cs, ys, hb, al, rl, gall, gt, at, gat, gm, co,
    hs, hin, so, sin, yin, ms, min, yin2, to, tin,
    rs_send, rs_recv, own, wsem, ssem, rsem,
):
    s = lax.axis_index("seq")
    c = lax.axis_index("chan")
    y = s // PLANE
    p = s % PLANE
    sib = (c // 2) * 2 + (1 - c % 2)
    far = (c + 2) % PARTS
    farsib = (sib + 2) % PARTS
    grad_scale = float(ROWS * PLANE * LAYERS) ** -0.5
    counter = [0]
    sends = []

    def plane(k):
        return (y * PLANE + (p + k) % PLANE, c)

    def layer(k):
        return (((y + k) % LAYERS) * PLANE + p, c)

    def ids(count):
        counter[0] += count
        return counter[0] - count

    def send(src, dst, device, slot):
        copy = pltpu.make_async_remote_copy(
            src_ref=src, dst_ref=dst, send_sem=ssem.at[slot], recv_sem=rsem.at[slot],
            device_id=device, device_id_type=MESH,
        )
        copy.start()
        sends.append(copy)
        return copy

    order = (c, sib, far, farsib)
    wcopies = []
    for n, h in enumerate(order):
        part = pl.ds(pl.multiple_of(h * DPART, DPART), DPART)
        copy = pltpu.make_async_copy(w_ref.at[part], wv.at[part], wsem.at[n])
        copy.start()
        wcopies.append(copy)

    barrier = pltpu.get_barrier_semaphore()
    greeted = [plane(k) for k in range(1, PLANE)] + [layer(k) for k in range(1, LAYERS)]
    greeted += [(s, sib), (s, far)]
    for device in greeted:
        pl.semaphore_signal(barrier, inc=1, device_id=device, device_id_type=MESH)

    for i in range(TILES):
        lanes = slice(128 * i, 128 * (i + 1))
        rate = rate_ref[:, lanes]
        al[pl.ds(i, MODES, stride=8), :] = jnp.exp(-rate)
        rl[pl.ds(i, MODES, stride=8), :] = res_ref[:, lanes] * jnp.sqrt(rate)
        x = (k_ref[:, lanes].astype(F32) * v_ref[:, lanes].astype(F32)).astype(BF16)
        xs[pl.ds(i, ROWS, stride=8), :] = x.astype(F32)

    def decay(m):
        return al[m * 8 : (m + 1) * 8, :]

    zero = jnp.zeros((8, 128), F32)

    def ahead(t, h):
        for u in range(4):
            x = xs[rows8(t * 4 + u), :]
            h = tuple(decay(m) * h[m] + x for m in range(MODES))
        return h

    h = lax.fori_loop(0, ROWS // 4, ahead, (zero,) * MODES)
    for m in range(MODES):
        hs[pl.ds(m, TILES, stride=MODES), :] = h[m]

    pl.semaphore_wait(barrier, len(greeted))

    def tile(index, size):
        return pl.ds(pl.multiple_of(index * size, size), size)

    slot = ids(PLANE - 1)
    h_in = [
        send(hs.at[tile((p + k) % PLANE, 16)], hin.at[tile(p, 16)], plane(k), slot + k - 1)
        for k in range(1, PLANE)
    ]
    slot = ids(3)
    g_far = send(g_ref, gall.at[c], (s, far), slot)
    g_sib = send(g_ref, gall.at[c], (s, sib), slot + 1)
    g_fwd_slot = slot + 2
    hin[tile(p, 16), :] = hs[tile(p, 16), :]
    gall[c] = g_ref[...]

    for k in range(PLANE):
        gt[k] = g_ref[:, PIECE * k : PIECE * (k + 1)].T
    slot = ids(PLANE - 1)
    mine = pl.ds(pl.multiple_of(p * ROWS, ROWS), ROWS)
    a_in = [
        send(gt.at[(p + k) % PLANE], at.at[c, :, mine], plane(k), slot + k - 1)
        for k in range(1, PLANE)
    ]
    at[c, :, mine] = gt[p]

    def mix(n, first):
        h = order[n]
        wcopies[n].wait()

        def step(j, carry):
            cols = pl.ds(pl.multiple_of(j * DEPTH, DEPTH), DEPTH)
            deep = pl.ds(pl.multiple_of(h * DPART + j * DEPTH, DEPTH), DEPTH)
            gm[...] += jnp.dot(gall[h, :, cols], wv[deep, :], preferred_element_type=F32)
            return carry

        lax.fori_loop(0, DPART // DEPTH, step, 0)

    gm[...] = jnp.zeros_like(gm)
    mix(0, True)

    my_tile = pl.ds(pl.multiple_of(p * 128, 128), 128)
    rate = rate_ref[:, my_tile]
    step_w = jnp.exp(-float(ROWS) * rate)
    layer_w = jnp.exp(-float(ROWS * PLANE) * rate)
    for copy in h_in:
        copy.wait_recv()
    state = jnp.zeros((MODES, 128), F32)
    for b in range(PLANE):
        so[b * 16 : (b + 1) * 16, :] = state
        state = step_w * state + hin[b * 16 : (b + 1) * 16, :]
    yin[tile(y, 16), :] = state
    slot = ids(LAYERS - 1)
    y_in = [
        send(yin.at[tile(y, 16)], yin.at[tile(y, 16)], layer(k), slot + k - 1)
        for k in range(1, LAYERS)
    ]
    g_sib.wait_recv()
    mix(1, False)
    for copy in y_in:
        copy.wait_recv()
    before = jnp.zeros((MODES, 128), F32)
    for b in range(LAYERS):
        before = jnp.where(b < y, layer_w * before + yin[b * 16 : (b + 1) * 16, :], before)
    for b in range(PLANE):
        so[b * 16 : (b + 1) * 16, :] += before
        before = step_w * before
    slot = ids(PLANE - 1)
    s_in = [
        send(so.at[tile((p + k) % PLANE, 16)], sin.at[tile(p, 16)], plane(k), slot + k - 1)
        for k in range(1, PLANE)
    ]
    sin[tile(p, 16), :] = so[tile(p, 16), :]

    for copy in a_in:
        copy.wait_recv()
    slot = ids(3)
    a_far = send(at.at[c], at.at[c], (s, far), slot)
    a_sib = send(at.at[c], at.at[c], (s, sib), slot + 1)
    a_fwd_slot = slot + 2
    g_far.wait_recv()
    g_fwd = send(gall.at[far], gall.at[far], (s, sib), g_fwd_slot)

    for copy in s_in:
        copy.wait_recv()

    def forward(t, h):
        for u in range(2):
            at_row = t * 2 + u
            x = xs[rows8(at_row), :]
            h = tuple(decay(m) * h[m] + x for m in range(MODES))
            terms = []
            for m in range(MODES):
                hb[rows8(at_row * MODES + m), :] = h[m]
                terms.append(rl[m * 8 : (m + 1) * 8, :] * h[m])
            while len(terms) > 1:
                terms = [terms[n] + terms[n + 1] for n in range(0, len(terms), 2)]
            ys[rows8(at_row), :] = terms[0]
        return h

    lax.fori_loop(
        0, ROWS // 2, forward,
        tuple(sin[pl.ds(m, TILES, stride=MODES), :] for m in range(MODES)),
    )
    gat_slot = ids(CHUNKS * (PLANE - 1))
    gat_in = []
    per = WIDE // 128
    for i in range(TILES):
        lanes = slice(128 * i, 128 * (i + 1))
        out = ys[pl.ds(i, ROWS, stride=8), :].astype(BF16)
        co[:, lanes] = out
        gated = (q_ref[:, lanes].astype(F32) * out.astype(F32)).astype(BF16)
        chunk, at_lane = i // per, i % per
        gat[chunk, mine, 128 * at_lane : 128 * (at_lane + 1)] = gated
        if at_lane == per - 1:
            gat_in.append([
                send(gat.at[chunk, mine], gat.at[chunk, mine], plane(k),
                     gat_slot + chunk * (PLANE - 1) + k - 1)
                for k in range(1, PLANE)
            ])

    mix(2, False)
    g_fwd.wait_recv()
    mix(3, False)
    for i in range(TILES):
        lanes = slice(128 * i, 128 * (i + 1))
        mixed = gm[:, lanes].astype(BF16).astype(F32)
        gq_ref[:, lanes] = (mixed * co[:, lanes].astype(F32)).astype(BF16)
        cot = (mixed * q_ref[:, lanes].astype(F32)).astype(BF16)
        cs[pl.ds(i, ROWS, stride=8), :] = cot.astype(F32)

    half = MODES // 2
    for part in range(2):
        modes = range(part * half, (part + 1) * half)

        def backward(n, carry, modes=modes):
            g, plain, ramp = carry
            for u in range(2):
                at_row = ROWS - 1 - (n * 2 + u)
                cot = cs[rows8(at_row), :]
                states = [hb[rows8(at_row * MODES + m), :] for m in modes]
                g = tuple(decay(m) * g[j] + cot for j, m in enumerate(modes))
                plain = tuple(plain[j] + states[j] * cot for j in range(half))
                ramp = tuple(ramp[j] + states[j] * g[j] for j in range(half))
            return g, plain, ramp

        found = lax.fori_loop(0, ROWS // 2, backward, ((zero,) * half,) * 3)
        for j, m in enumerate(modes):
            for n in range(3):
                ms[pl.ds(n * 16 + m, TILES, stride=64), :] = found[n][j]

    def reach(t, z):
        for u in range(2):
            z = tuple(
                decay(m) * (z[m] + hb[rows8((t * 2 + u) * MODES + m), :]) for m in range(MODES)
            )
        return z

    z = lax.fori_loop(0, ROWS // 2, reach, (zero,) * MODES)
    for m in range(MODES):
        ms[pl.ds(48 + m, TILES, stride=64), :] = z[m]
    slot = ids(PLANE - 1)
    m_in = [
        send(ms.at[tile((p + k) % PLANE, 64)], min.at[tile(p, 64)], plane(k), slot + k - 1)
        for k in range(1, PLANE)
    ]
    min[tile(p, 64), :] = ms[tile(p, 64), :]

    a_far.wait_recv()
    a_fwd = send(at.at[far], at.at[far], (s, sib), a_fwd_slot)
    a_sib.wait_recv()
    a_fwd.wait_recv()

    rs_slot = ids(CHUNKS * (LAYERS - 1))
    rs_in = []

    def product(chunk):
        for copy in gat_in[chunk]:
            copy.wait_recv()
        for k in range(1, LAYERS):
            there = (y + k) % LAYERS
            value = jnp.dot(at[there], gat[chunk], preferred_element_type=F32)
            rs_send[chunk, k - 1] = value.astype(BF16)
            rs_in.append(
                send(rs_send.at[chunk, k - 1], rs_recv.at[chunk, k - 1], layer(k),
                     rs_slot + chunk * (LAYERS - 1) + k - 1)
            )
        own[:, chunk * WIDE : (chunk + 1) * WIDE] = jnp.dot(
            at[y], gat[chunk], preferred_element_type=F32
        )

    product(0)

    for copy in m_in:
        copy.wait_recv()
    blank = jnp.zeros((MODES, 128), F32)
    state, plain, ramp, carried, power = blank, blank, blank, blank, blank + 1.0
    for b in reversed(range(PLANE)):
        g_b, p_b, q_b, z_b = (min[b * 64 + n * 16 : b * 64 + (n + 1) * 16, :] for n in range(4))
        to[b * 48 : b * 48 + 16, :] = state
        plain = plain + p_b
        ramp = ramp + q_b + state * z_b
        carried = carried + power * z_b
        state = step_w * state + g_b
        power = power * step_w
    here = y * 64
    for n, value in enumerate((state, plain, ramp, carried)):
        yin2[pl.ds(pl.multiple_of(here + n * 16, 16), 16), :] = value
    slot = ids(LAYERS - 1)
    y2_in = [
        send(yin2.at[tile(y, 64)], yin2.at[tile(y, 64)], layer(k), slot + k - 1)
        for k in range(1, LAYERS)
    ]

    product(1)

    for copy in y2_in:
        copy.wait_recv()
    after, chosen, plain, ramp = blank, blank, blank, blank
    for b in reversed(range(LAYERS)):
        g_b, p_b, q_b, z_b = (yin2[b * 64 + n * 16 : b * 64 + (n + 1) * 16, :] for n in range(4))
        plain = plain + p_b
        ramp = ramp + q_b + after * z_b
        chosen = jnp.where(b == y, after, chosen)
        after = layer_w * after + g_b
    root = jnp.sqrt(rate) * grad_scale
    grad_res = root * plain
    grad_log = res_ref[:, my_tile] * root * (0.5 * plain - rate * (ramp - plain))
    for b in reversed(range(PLANE)):
        to[b * 48 : b * 48 + 16, :] += chosen
        chosen = step_w * chosen
        to[b * 48 + 16 : b * 48 + 32, :] = grad_res
        to[b * 48 + 32 : b * 48 + 48, :] = grad_log
    slot = ids(PLANE - 1)
    t_in = [
        send(to.at[tile((p + k) % PLANE, 48)], tin.at[tile(p, 48)], plane(k), slot + k - 1)
        for k in range(1, PLANE)
    ]
    tin[tile(p, 48), :] = to[tile(p, 48), :]

    product(2)

    for copy in t_in:
        copy.wait_recv()
    for i in range(TILES):
        lanes = slice(128 * i, 128 * (i + 1))
        gr_ref[:, lanes] = tin[i * 48 + 16 : i * 48 + 32, :]
        gl_ref[:, lanes] = tin[i * 48 + 32 : i * 48 + 48, :]

    def final(n, g):
        for u in range(2):
            at_row = ROWS - 1 - (n * 2 + u)
            cot = cs[rows8(at_row), :]
            g = tuple(decay(m) * g[m] + cot for m in range(MODES))
            terms = [rl[m * 8 : (m + 1) * 8, :] * g[m] for m in range(MODES)]
            while len(terms) > 1:
                terms = [terms[n] + terms[n + 1] for n in range(0, len(terms), 2)]
            ys[rows8(at_row), :] = terms[0]
        return g

    lax.fori_loop(
        0, ROWS // 2, final,
        tuple(tin[pl.ds(m, TILES, stride=48), :] for m in range(MODES)),
    )
    for i in range(TILES):
        lanes = slice(128 * i, 128 * (i + 1))
        back = ys[pl.ds(i, ROWS, stride=8), :].astype(BF16).astype(F32)
        gk_ref[:, lanes] = (back * v_ref[:, lanes].astype(F32)).astype(BF16)
        gv_ref[:, lanes] = (back * k_ref[:, lanes].astype(F32)).astype(BF16)

    product(3)

    for copy in rs_in:
        copy.wait_recv()
    for chunk in range(CHUNKS):
        cols = slice(chunk * WIDE, (chunk + 1) * WIDE)
        total = own[:, cols]
        for k in range(LAYERS - 1):
            total = total + rs_recv[chunk, k].astype(F32)
        gw_ref[:, cols] = total * grad_scale
    for copy in sends:
        copy.wait_send()
    assert counter[0] <= SLOTS


SLOTS = 96


def per_device(query_act, key_act, value_act, residue, decay_rate, out_weight, grad_out):
    vmem = pl.BlockSpec(memory_space=pltpu.VMEM)
    shape = jax.ShapeDtypeStruct
    small = shape((ROWS, COLS), BF16)
    modal = shape((MODES, COLS), F32)
    scratch = [
        ((PARTS * DPART, COLS), BF16),
        ((ROWS * 8, 128), F32),
        ((ROWS * 8, 128), F32),
        ((ROWS * 8, 128), F32),
        ((ROWS * MODES * 8, 128), F32),
        ((MODES * 8, 128), F32),
        ((MODES * 8, 128), F32),
        ((PARTS, ROWS, DPART), BF16),
        ((PLANE, PIECE, ROWS), BF16),
        ((PARTS, PIECE, PLANE * ROWS), BF16),
        ((CHUNKS, PLANE * ROWS, WIDE), BF16),
        ((ROWS, COLS), F32),
        ((ROWS, COLS), BF16),
        ((TILES * 16, 128), F32),
        ((PLANE * 16, 128), F32),
        ((PLANE * 16, 128), F32),
        ((TILES * 16, 128), F32),
        ((LAYERS * 16, 128), F32),
        ((TILES * 64, 128), F32),
        ((PLANE * 64, 128), F32),
        ((LAYERS * 64, 128), F32),
        ((PLANE * 48, 128), F32),
        ((TILES * 48, 128), F32),
        ((CHUNKS, LAYERS - 1, PIECE, WIDE), BF16),
        ((CHUNKS, LAYERS - 1, PIECE, WIDE), BF16),
        ((PIECE, COLS), F32),
    ]
    return pl.pallas_call(
        body,
        out_shape=(small, small, small, shape((PIECE, COLS), F32), modal, modal),
        in_specs=[vmem] * 6 + [pl.BlockSpec(memory_space=pl.ANY)],
        out_specs=(vmem,) * 6,
        scratch_shapes=[pltpu.VMEM(*entry) for entry in scratch]
        + [
            pltpu.SemaphoreType.DMA((4,)),
            pltpu.SemaphoreType.DMA((SLOTS,)),
            pltpu.SemaphoreType.DMA((SLOTS,)),
        ],
        compiler_params=pltpu.CompilerParams(
            collective_id=0, has_side_effects=True, vmem_limit_bytes=56 * 2**20
        ),
        cost_estimate=pl.CostEstimate(
            flops=2 * 2**31, bytes_accessed=20 * 2**20, transcendentals=0
        ),
    )(query_act, key_act, value_act, grad_out, residue, decay_rate, out_weight)


def solution(mesh):
    both = P("seq", "chan")
    chan = P(None, "chan")
    return jax.shard_map(
        per_device,
        mesh=mesh,
        in_specs=(both, both, both, chan, chan, chan, both),
        out_specs=(both, both, both, both, chan, chan),
        check_vma=False,
    )
```

```python
import jax
import jax.numpy as jnp
from jax import lax
from jax.experimental import pallas as pl
from jax.experimental.pallas import tpu as pltpu
from jax.sharding import PartitionSpec as P

MESH = pl.DeviceIdType.MESH
F32 = jnp.float32
BF16 = jnp.bfloat16
ROWS = 128
COLS = 1024
TILES = 8
MODES = 16
PLANE = 8
LAYERS = 4
PARTS = 4
DPART = 2048
PIECE = 256
CHUNKS = 4
WIDE = COLS // CHUNKS
DEPTH = 512


def rows8(index):
    return pl.ds(pl.multiple_of(index * 8, 8), 8)


def body(
    q_ref, k_ref, v_ref, g_ref, res_ref, rate_ref, w_ref,
    gq_ref, gk_ref, gv_ref, gw_ref, gr_ref, gl_ref,
    wv, xs, cs, ys, hb, al, rl, gall, gt, turned, at, gat, gm, co,
    hs, hin, so, sin, yin, ms, min, yin2, to, tin,
    rs_send, rs_recv, own, wsem, ssem, rsem,
):
    s = lax.axis_index("seq")
    c = lax.axis_index("chan")
    y = s // PLANE
    p = s % PLANE
    sib = (c // 2) * 2 + (1 - c % 2)
    far = (c + 2) % PARTS
    farsib = (sib + 2) % PARTS
    grad_scale = float(ROWS * PLANE * LAYERS) ** -0.5
    counter = [0]
    sends = []

    def plane(k):
        return (y * PLANE + (p + k) % PLANE, c)

    def across(k):
        return (y * PLANE + (p + 2 * k) % PLANE, c)

    def place(x_step, z_turn):
        return ((p // 2 + x_step) % 4) * 2 + (p % 2 + z_turn) % 2

    def layer(k):
        return (((y + k) % LAYERS) * PLANE + p, c)

    def ids(count):
        counter[0] += count
        return counter[0] - count

    def send(src, dst, device, slot):
        copy = pltpu.make_async_remote_copy(
            src_ref=src, dst_ref=dst, send_sem=ssem.at[slot], recv_sem=rsem.at[slot],
            device_id=device, device_id_type=MESH,
        )
        copy.start()
        sends.append(copy)
        return copy

    order = (c, sib, far, farsib)
    wcopies = []
    for n, h in enumerate(order):
        part = pl.ds(pl.multiple_of(h * DPART, DPART), DPART)
        copy = pltpu.make_async_copy(w_ref.at[part], wv.at[part], wsem.at[n])
        copy.start()
        wcopies.append(copy)

    barrier = pltpu.get_barrier_semaphore()
    greeted = [plane(k) for k in range(1, PLANE)] + [layer(k) for k in range(1, LAYERS)]
    greeted += [(s, sib), (s, far)]
    greeted += [(y * PLANE + place(k, 1), far) for k in range(4)]
    for device in greeted:
        pl.semaphore_signal(barrier, inc=1, device_id=device, device_id_type=MESH)

    for i in range(TILES):
        lanes = slice(128 * i, 128 * (i + 1))
        rate = rate_ref[:, lanes]
        al[pl.ds(i, MODES, stride=8), :] = jnp.exp(-rate)
        rl[pl.ds(i, MODES, stride=8), :] = res_ref[:, lanes] * jnp.sqrt(rate)
        x = (k_ref[:, lanes].astype(F32) * v_ref[:, lanes].astype(F32)).astype(BF16)
        xs[pl.ds(i, ROWS, stride=8), :] = x.astype(F32)

    def decay(m):
        return al[m * 8 : (m + 1) * 8, :]

    zero = jnp.zeros((8, 128), F32)

    def ahead(t, h):
        for u in range(4):
            x = xs[rows8(t * 4 + u), :]
            h = tuple(decay(m) * h[m] + x for m in range(MODES))
        return h

    h = lax.fori_loop(0, ROWS // 4, ahead, (zero,) * MODES)
    for m in range(MODES):
        hs[pl.ds(m, TILES, stride=MODES), :] = h[m]

    pl.semaphore_wait(barrier, len(greeted))

    def tile(index, size):
        return pl.ds(pl.multiple_of(index * size, size), size)

    slot = ids(PLANE - 1)
    h_in = [
        send(hs.at[tile((p + k) % PLANE, 16)], hin.at[tile(p, 16)], plane(k), slot + k - 1)
        for k in range(1, PLANE)
    ]
    slot = ids(9)
    g_sib = send(g_ref, gall.at[c], (s, sib), slot)

    g_slot = slot

    def far_part(j):
        cols = pl.ds(j * DEPTH, DEPTH)
        return send(g_ref.at[:, cols], gall.at[c, :, cols], (s, far), g_slot + 1 + j)

    def far_pass(j):
        cols = pl.ds(j * DEPTH, DEPTH)
        g_far[j].wait_recv()
        return send(gall.at[far, :, cols], gall.at[far, :, cols], (s, sib), g_slot + 5 + j)

    g_far = [far_part(0), far_part(1)]
    hin[tile(p, 16), :] = hs[tile(p, 16), :]
    gall[c] = g_ref[...]

    for k in range(PLANE):
        gt[k] = g_ref[:, PIECE * k : PIECE * (k + 1)].T
    slot = ids(11)
    a_slot = slot
    mine = pl.ds(pl.multiple_of(p * ROWS, ROWS), ROWS)
    a_near = [
        send(gt.at[place(k, 0)], at.at[c, :, mine], across(k), slot + k - 1) for k in range(1, 4)
    ]
    at[c, :, mine] = gt[p]

    def mix(n, first):
        h = order[n]
        wcopies[n].wait()

        def step(j, carry):
            cols = pl.ds(pl.multiple_of(j * DEPTH, DEPTH), DEPTH)
            deep = pl.ds(pl.multiple_of(h * DPART + j * DEPTH, DEPTH), DEPTH)
            gm[...] += jnp.dot(gall[h, :, cols], wv[deep, :], preferred_element_type=F32)
            return carry

        lax.fori_loop(0, DPART // DEPTH, step, 0)

    gm[...] = jnp.zeros_like(gm)
    mix(0, True)

    my_tile = pl.ds(pl.multiple_of(p * 128, 128), 128)
    rate = rate_ref[:, my_tile]
    step_w = jnp.exp(-float(ROWS) * rate)
    layer_w = jnp.exp(-float(ROWS * PLANE) * rate)
    for copy in h_in:
        copy.wait_recv()
    state = jnp.zeros((MODES, 128), F32)
    for b in range(PLANE):
        so[b * 16 : (b + 1) * 16, :] = state
        state = step_w * state + hin[b * 16 : (b + 1) * 16, :]
    yin[tile(y, 16), :] = state
    slot = ids(LAYERS - 1)
    y_in = [
        send(yin.at[tile(y, 16)], yin.at[tile(y, 16)], layer(k), slot + k - 1)
        for k in range(1, LAYERS)
    ]
    g_sib.wait_recv()
    mix(1, False)
    for copy in y_in:
        copy.wait_recv()
    before = jnp.zeros((MODES, 128), F32)
    for b in range(LAYERS):
        before = jnp.where(b < y, layer_w * before + yin[b * 16 : (b + 1) * 16, :], before)
    for b in range(PLANE):
        so[b * 16 : (b + 1) * 16, :] += before
        before = step_w * before
    slot = ids(PLANE - 1)
    s_in = [
        send(so.at[tile((p + k) % PLANE, 16)], sin.at[tile(p, 16)], plane(k), slot + k - 1)
        for k in range(1, PLANE)
    ]
    sin[tile(p, 16), :] = so[tile(p, 16), :]

    g_far += [far_part(2), far_part(3)]
    g_pass = [far_pass(0), far_pass(1)]

    for copy in s_in:
        copy.wait_recv()

    def forward(t, h):
        for u in range(2):
            at_row = t * 2 + u
            x = xs[rows8(at_row), :]
            h = tuple(decay(m) * h[m] + x for m in range(MODES))
            terms = []
            for m in range(MODES):
                hb[rows8(at_row * MODES + m), :] = h[m]
                terms.append(rl[m * 8 : (m + 1) * 8, :] * h[m])
            while len(terms) > 1:
                terms = [terms[n] + terms[n + 1] for n in range(0, len(terms), 2)]
            ys[rows8(at_row), :] = terms[0]
        return h

    lax.fori_loop(
        0, ROWS // 2, forward,
        tuple(sin[pl.ds(m, TILES, stride=MODES), :] for m in range(MODES)),
    )
    per = WIDE // 128
    for i in range(TILES):
        lanes = slice(128 * i, 128 * (i + 1))
        out = ys[pl.ds(i, ROWS, stride=8), :].astype(BF16)
        co[:, lanes] = out
        gated = (q_ref[:, lanes].astype(F32) * out.astype(F32)).astype(BF16)
        chunk, at_lane = i // per, i % per
        gat[chunk, mine, 128 * at_lane : 128 * (at_lane + 1)] = gated

    gat_slot = ids(CHUNKS * (PLANE - 1))
    other = place(0, 1)
    theirs = pl.ds(pl.multiple_of(other * ROWS, ROWS), ROWS)
    gat_z, gat_in = [], []

    def spread(chunk):
        slot = gat_slot + chunk * (PLANE - 1)
        block = gat.at[chunk, mine]
        gat_z.append(send(block, block, (y * PLANE + other, c), slot))
        gat_in.append([send(block, block, across(k), slot + k) for k in (1, 3, 2)])

    def spread_more(chunk):
        slot = gat_slot + chunk * (PLANE - 1) + 3
        block = gat.at[chunk, theirs]
        gat_z[chunk].wait_recv()
        gat_in[chunk] += [send(block, block, across(k), slot + k) for k in (1, 3, 2)]

    spread(0)

    a_near += [
        send(gt.at[place(k, 1)], at.at[c, :, mine], (y * PLANE + place(k, 1), c), a_slot + 3 + k)
        for k in range(4)
    ]
    a_cross = [
        send(gt.at[place(k, 1)], at.at[c, :, mine], (y * PLANE + place(k, 1), far), a_slot + 7 + k)
        for k in range(4)
    ]

    g_pass += [far_pass(2), far_pass(3)]
    mix(2, False)
    spread_more(0)
    for copy in g_pass:
        copy.wait_recv()
    mix(3, False)
    for i in range(TILES):
        lanes = slice(128 * i, 128 * (i + 1))
        mixed = gm[:, lanes].astype(BF16).astype(F32)
        gq_ref[:, lanes] = (mixed * co[:, lanes].astype(F32)).astype(BF16)
        cot = (mixed * q_ref[:, lanes].astype(F32)).astype(BF16)
        cs[pl.ds(i, ROWS, stride=8), :] = cot.astype(F32)

    half = MODES // 2
    for part in range(2):
        modes = range(part * half, (part + 1) * half)

        def backward(n, carry, modes=modes):
            g, plain, ramp = carry
            for u in range(2):
                at_row = ROWS - 1 - (n * 2 + u)
                cot = cs[rows8(at_row), :]
                states = [hb[rows8(at_row * MODES + m), :] for m in modes]
                g = tuple(decay(m) * g[j] + cot for j, m in enumerate(modes))
                plain = tuple(plain[j] + states[j] * cot for j in range(half))
                ramp = tuple(ramp[j] + states[j] * g[j] for j in range(half))
            return g, plain, ramp

        found = lax.fori_loop(0, ROWS // 2, backward, ((zero,) * half,) * 3)
        for j, m in enumerate(modes):
            for n in range(3):
                ms[pl.ds(n * 16 + m, TILES, stride=64), :] = found[n][j]

    def reach(t, z):
        for u in range(2):
            z = tuple(
                decay(m) * (z[m] + hb[rows8((t * 2 + u) * MODES + m), :]) for m in range(MODES)
            )
        return z

    z = lax.fori_loop(0, ROWS // 2, reach, (zero,) * MODES)
    for m in range(MODES):
        ms[pl.ds(48 + m, TILES, stride=64), :] = z[m]
    slot = ids(PLANE - 1)
    m_in = [
        send(ms.at[tile((p + k) % PLANE, 64)], min.at[tile(p, 64)], plane(k), slot + k - 1)
        for k in range(1, PLANE)
    ]
    min[tile(p, 64), :] = ms[tile(p, 64), :]

    slot = ids(5)
    for k in range(4):
        turned[k] = gall[far, :, pl.ds(pl.multiple_of(place(k, 0) * PIECE, PIECE), PIECE)].T
    a_cross += [
        send(turned.at[k], at.at[far, :, mine], across(k), slot + k - 1) for k in range(1, 4)
    ]
    at[far, :, mine] = turned[0]
    spread(1)
    for copy in a_near:
        copy.wait_recv()
    a_sib = [send(at.at[c], at.at[c], (s, sib), slot + 3)]
    for copy in a_cross:
        copy.wait_recv()
    a_sib.append(send(at.at[far], at.at[far], (s, sib), slot + 4))
    spread_more(1)

    rs_slot = ids(CHUNKS * (LAYERS - 1))
    rs_in = []

    def product(chunk):
        for copy in gat_in[chunk]:
            copy.wait_recv()
        for k in range(1, LAYERS):
            there = (y + k) % LAYERS
            value = jnp.dot(at[there], gat[chunk], preferred_element_type=F32)
            rs_send[chunk, k - 1] = value.astype(BF16)
            rs_in.append(
                send(rs_send.at[chunk, k - 1], rs_recv.at[chunk, k - 1], layer(k),
                     rs_slot + chunk * (LAYERS - 1) + k - 1)
            )
        own[:, chunk * WIDE : (chunk + 1) * WIDE] = jnp.dot(
            at[y], gat[chunk], preferred_element_type=F32
        )

    for copy in m_in:
        copy.wait_recv()
    blank = jnp.zeros((MODES, 128), F32)
    state, plain, ramp, carried, power = blank, blank, blank, blank, blank + 1.0
    for b in reversed(range(PLANE)):
        g_b, p_b, q_b, z_b = (min[b * 64 + n * 16 : b * 64 + (n + 1) * 16, :] for n in range(4))
        to[b * 48 : b * 48 + 16, :] = state
        plain = plain + p_b
        ramp = ramp + q_b + state * z_b
        carried = carried + power * z_b
        state = step_w * state + g_b
        power = power * step_w
    here = y * 64
    for n, value in enumerate((state, plain, ramp, carried)):
        yin2[pl.ds(pl.multiple_of(here + n * 16, 16), 16), :] = value
    slot = ids(LAYERS - 1)
    y2_in = [
        send(yin2.at[tile(y, 64)], yin2.at[tile(y, 64)], layer(k), slot + k - 1)
        for k in range(1, LAYERS)
    ]

    for copy in a_sib:
        copy.wait_recv()
    product(0)
    spread(2)

    for copy in y2_in:
        copy.wait_recv()
    after, chosen, plain, ramp = blank, blank, blank, blank
    for b in reversed(range(LAYERS)):
        g_b, p_b, q_b, z_b = (yin2[b * 64 + n * 16 : b * 64 + (n + 1) * 16, :] for n in range(4))
        plain = plain + p_b
        ramp = ramp + q_b + after * z_b
        chosen = jnp.where(b == y, after, chosen)
        after = layer_w * after + g_b
    root = jnp.sqrt(rate) * grad_scale
    grad_res = root * plain
    grad_log = res_ref[:, my_tile] * root * (0.5 * plain - rate * (ramp - plain))
    for b in reversed(range(PLANE)):
        to[b * 48 : b * 48 + 16, :] += chosen
        chosen = step_w * chosen
        to[b * 48 + 16 : b * 48 + 32, :] = grad_res
        to[b * 48 + 32 : b * 48 + 48, :] = grad_log
    slot = ids(PLANE - 1)
    t_in = [
        send(to.at[tile((p + k) % PLANE, 48)], tin.at[tile(p, 48)], plane(k), slot + k - 1)
        for k in range(1, PLANE)
    ]
    tin[tile(p, 48), :] = to[tile(p, 48), :]

    product(1)
    spread_more(2)
    spread(3)

    for copy in t_in:
        copy.wait_recv()
    for i in range(TILES):
        lanes = slice(128 * i, 128 * (i + 1))
        gr_ref[:, lanes] = tin[i * 48 + 16 : i * 48 + 32, :]
        gl_ref[:, lanes] = tin[i * 48 + 32 : i * 48 + 48, :]

    def final(n, g):
        for u in range(2):
            at_row = ROWS - 1 - (n * 2 + u)
            cot = cs[rows8(at_row), :]
            g = tuple(decay(m) * g[m] + cot for m in range(MODES))
            terms = [rl[m * 8 : (m + 1) * 8, :] * g[m] for m in range(MODES)]
            while len(terms) > 1:
                terms = [terms[n] + terms[n + 1] for n in range(0, len(terms), 2)]
            ys[rows8(at_row), :] = terms[0]
        return g

    lax.fori_loop(
        0, ROWS // 2, final,
        tuple(tin[pl.ds(m, TILES, stride=48), :] for m in range(MODES)),
    )
    for i in range(TILES):
        lanes = slice(128 * i, 128 * (i + 1))
        back = ys[pl.ds(i, ROWS, stride=8), :].astype(BF16).astype(F32)
        gk_ref[:, lanes] = (back * v_ref[:, lanes].astype(F32)).astype(BF16)
        gv_ref[:, lanes] = (back * k_ref[:, lanes].astype(F32)).astype(BF16)

    spread_more(3)
    product(2)
    product(3)

    for copy in rs_in:
        copy.wait_recv()
    for chunk in range(CHUNKS):
        cols = slice(chunk * WIDE, (chunk + 1) * WIDE)
        total = own[:, cols]
        for k in range(LAYERS - 1):
            total = total + rs_recv[chunk, k].astype(F32)
        gw_ref[:, cols] = total * grad_scale
    for copy in sends:
        copy.wait_send()
    assert counter[0] <= SLOTS


SLOTS = 112


def settle(*refs):
    count = len(refs) // 2
    for n in range(count):
        refs[count + n][...] = refs[n][...]


def per_device(query_act, key_act, value_act, residue, decay_rate, out_weight, grad_out):
    vmem = pl.BlockSpec(memory_space=pltpu.VMEM)
    shape = jax.ShapeDtypeStruct
    small = shape((ROWS, COLS), BF16)
    modal = shape((MODES, COLS), F32)
    scratch = [
        ((PARTS * DPART, COLS), BF16),
        ((ROWS * 8, 128), F32),
        ((ROWS * 8, 128), F32),
        ((ROWS * 8, 128), F32),
        ((ROWS * MODES * 8, 128), F32),
        ((MODES * 8, 128), F32),
        ((MODES * 8, 128), F32),
        ((PARTS, ROWS, DPART), BF16),
        ((PLANE, PIECE, ROWS), BF16),
        ((4, PIECE, ROWS), BF16),
        ((PARTS, PIECE, PLANE * ROWS), BF16),
        ((CHUNKS, PLANE * ROWS, WIDE), BF16),
        ((ROWS, COLS), F32),
        ((ROWS, COLS), BF16),
        ((TILES * 16, 128), F32),
        ((PLANE * 16, 128), F32),
        ((PLANE * 16, 128), F32),
        ((TILES * 16, 128), F32),
        ((LAYERS * 16, 128), F32),
        ((TILES * 64, 128), F32),
        ((PLANE * 64, 128), F32),
        ((LAYERS * 64, 128), F32),
        ((PLANE * 48, 128), F32),
        ((TILES * 48, 128), F32),
        ((CHUNKS, LAYERS - 1, PIECE, WIDE), BF16),
        ((CHUNKS, LAYERS - 1, PIECE, WIDE), BF16),
        ((PIECE, COLS), F32),
    ]
    outs = (small, small, small, shape((PIECE, COLS), F32), modal, modal)
    found = pl.pallas_call(
        body,
        out_shape=outs,
        in_specs=[vmem] * 6 + [pl.BlockSpec(memory_space=pl.ANY)],
        out_specs=(vmem,) * 6,
        scratch_shapes=[pltpu.VMEM(*entry) for entry in scratch]
        + [
            pltpu.SemaphoreType.DMA((4,)),
            pltpu.SemaphoreType.DMA((SLOTS,)),
            pltpu.SemaphoreType.DMA((SLOTS,)),
        ],
        compiler_params=pltpu.CompilerParams(
            collective_id=0, has_side_effects=True, vmem_limit_bytes=56 * 2**20
        ),
        cost_estimate=pl.CostEstimate(
            flops=2 * 2**31, bytes_accessed=20 * 2**20, transcendentals=0
        ),
    )(query_act, key_act, value_act, grad_out, residue, decay_rate, out_weight)
    return pl.pallas_call(
        settle,
        out_shape=outs,
        in_specs=[vmem] * len(outs),
        out_specs=(vmem,) * len(outs),
    )(*found)


def solution(mesh):
    both = P("seq", "chan")
    chan = P(None, "chan")
    return jax.shard_map(
        per_device,
        mesh=mesh,
        in_specs=(both, both, both, chan, chan, chan, both),
        out_specs=(both, both, both, both, chan, chan),
        check_vma=False,
    )
```

```python
import jax
import jax.numpy as jnp
from jax import lax
from jax.experimental import pallas as pl
from jax.experimental.pallas import tpu as pltpu
from jax.sharding import PartitionSpec as P

MESH = pl.DeviceIdType.MESH
F32 = jnp.float32
BF16 = jnp.bfloat16
ROWS = 128
COLS = 1024
TILES = 8
MODES = 16
PLANE = 8
LAYERS = 4
PARTS = 4
DPART = 2048
PIECE = 256
WIDTHS = (256, 256, 256, 128, 128)
CHUNKS = len(WIDTHS)
RELAYED = 3
DEPTH = 512


def rows8(index):
    return pl.ds(pl.multiple_of(index * 8, 8), 8)


def body(
    q_hbm, k_hbm, v_hbm, g_hbm, res_hbm, rate_hbm, w_ref,
    gq_ref, gk_ref, gv_ref, gw_ref, gr_ref, gl_ref,
    q_ref, k_ref, v_ref, g_ref, res_ref, rate_ref,
    wv, xs, cs, ys, hb, al, rl, gall, gt, turned, at, gat, gm, co,
    hs, hin, so, sin, yin, gs, gin, yin2, to, tin, pq, pin, yp, pr, prin,
    rs_send, rs_recv, relay_send, relay_recv, held, own, wsem, ssem, rsem,
):
    s = lax.axis_index("seq")
    c = lax.axis_index("chan")
    y = s // PLANE
    p = s % PLANE
    sib = (c // 2) * 2 + (1 - c % 2)
    far = (c + 2) % PARTS
    farsib = (sib + 2) % PARTS
    grad_scale = float(ROWS * PLANE * LAYERS) ** -0.5
    counter = [0]
    sends = []

    def plane(k):
        return (y * PLANE + (p + k) % PLANE, c)

    def across(k):
        return (y * PLANE + (p + 2 * k) % PLANE, c)

    def place(x_step, z_turn):
        return ((p // 2 + x_step) % 4) * 2 + (p % 2 + z_turn) % 2

    def layer(k):
        return (((y + k) % LAYERS) * PLANE + p, c)

    def ids(count):
        counter[0] += count
        assert counter[0] <= SLOTS
        return counter[0] - count

    def send(src, dst, device, slot):
        copy = pltpu.make_async_remote_copy(
            src_ref=src, dst_ref=dst, send_sem=ssem.at[slot], recv_sem=rsem.at[slot],
            device_id=device, device_id_type=MESH,
        )
        copy.start()
        sends.append(copy)
        return copy

    def tile(index, size):
        return pl.ds(pl.multiple_of(index * size, size), size)

    def decay(m):
        return al[m * 8 : (m + 1) * 8, :]

    def amplitude(m):
        return rl[m * 8 : (m + 1) * 8, :]

    def tree(terms):
        while len(terms) > 1:
            terms = [terms[n] + terms[n + 1] for n in range(0, len(terms), 2)]
        return terms[0]

    barrier = pltpu.get_barrier_semaphore()
    greeted = [plane(k) for k in range(1, PLANE)] + [layer(k) for k in range(1, LAYERS)]
    greeted += [(s, sib), (s, far)]
    greeted += [(y * PLANE + place(k, 1), far) for k in range(4)]
    for device in greeted:
        pl.semaphore_signal(barrier, inc=1, device_id=device, device_id_type=MESH)

    loads = {}
    for n, (name, src, dst) in enumerate((
        ("rate", rate_hbm, rate_ref), ("k", k_hbm, k_ref), ("v", v_hbm, v_ref),
        ("res", res_hbm, res_ref), ("g", g_hbm, g_ref), ("q", q_hbm, q_ref),
    )):
        loads[name] = pltpu.make_async_copy(src, dst, wsem.at[PARTS + n])
        loads[name].start()
    order = (c, sib, far, farsib)
    wcopies = []
    for n, h in enumerate(order):
        part = tile(h, DPART)
        copy = pltpu.make_async_copy(w_ref.at[part], wv.at[part], wsem.at[n])
        copy.start()
        wcopies.append(copy)

    for name in ("rate", "k", "v"):
        loads[name].wait()
    for i in range(TILES):
        lanes = slice(128 * i, 128 * (i + 1))
        al[pl.ds(i, MODES, stride=8), :] = jnp.exp(-rate_ref[:, lanes])
        x = (k_ref[:, lanes].astype(F32) * v_ref[:, lanes].astype(F32)).astype(BF16)
        xs[pl.ds(i, ROWS, stride=8), :] = x.astype(F32)

    zero = jnp.zeros((8, 128), F32)

    def ahead(t, h):
        for u in range(4):
            x = xs[rows8(t * 4 + u), :]
            h = tuple(decay(m) * h[m] + x for m in range(MODES))
        return h

    h = lax.fori_loop(0, ROWS // 4, ahead, (zero,) * MODES)
    for m in range(MODES):
        hs[pl.ds(m, TILES, stride=MODES), :] = h[m]

    pl.semaphore_wait(barrier, len(greeted))

    def to_owners(src, dst, size):
        slot = ids(PLANE - 1)
        copies = [
            send(src.at[tile((p + k) % PLANE, size)], dst.at[tile(p, size)], plane(k), slot + k - 1)
            for k in range(1, PLANE)
        ]
        dst[tile(p, size), :] = src[tile(p, size), :]
        return copies

    def to_layers(ref, size):
        slot = ids(LAYERS - 1)
        block = ref.at[tile(y, size)]
        return [send(block, block, layer(k), slot + k - 1) for k in range(1, LAYERS)]

    def arrive(copies):
        for copy in copies:
            copy.wait_recv()

    h_in = to_owners(hs, hin, 16)
    loads["g"].wait()
    g_slot = ids(9)
    g_sib = send(g_ref, gall.at[c], (s, sib), g_slot)

    def far_cols(n):
        return tile((p // 2 + n) % 4, DEPTH)

    def far_part(n):
        cols = far_cols(n)
        g_far[n] = send(g_ref.at[:, cols], gall.at[c, :, cols], (s, far), g_slot + 1 + n)

    def far_pass(n):
        cols = far_cols(n)
        g_far[n].wait_recv()
        block = gall.at[far, :, cols]
        g_pass[n] = send(block, block, (s, sib), g_slot + 5 + n)
        turned[n] = gall[far, :, tile(place(n, 0), PIECE)].T
        if n == 0:
            at[far, :, mine] = turned[0]
        else:
            a_cross.append(
                send(turned.at[n], at.at[far, :, mine], across(n), a_slot + 10 + n)
            )
        mix(2, n)

    g_far, g_pass = {}, {}
    gall[c] = g_ref[...]

    for k in range(PLANE):
        gt[k] = g_ref[:, PIECE * k : PIECE * (k + 1)].T
    a_slot = ids(16)
    mine = tile(p, ROWS)
    a_near = [
        send(gt.at[place(k, 0)], at.at[c, :, mine], across(k), a_slot + k - 1) for k in range(1, 4)
    ]
    at[c, :, mine] = gt[p]
    a_near += [
        send(gt.at[place(k, 1)], at.at[c, :, mine], (y * PLANE + place(k, 1), c), a_slot + 3 + k)
        for k in range(4)
    ]
    a_cross = [
        send(gt.at[place(k, 1)], at.at[c, :, mine], (y * PLANE + place(k, 1), far), a_slot + 7 + k)
        for k in range(4)
    ]
    far_part(1)

    seen = set()

    def mix(n, j):
        h = order[n]
        if n not in seen:
            seen.add(n)
            wcopies[n].wait()
        if n >= 2:
            j = (p // 2 + j) % 4
        deep = pl.ds(pl.multiple_of(h * DPART + j * DEPTH, DEPTH), DEPTH)
        cols = tile(j, DEPTH)
        gm[...] += jnp.dot(gall[h, :, cols], wv[deep, :], preferred_element_type=F32)

    gm[...] = jnp.zeros_like(gm)
    loads["res"].wait()
    for i in range(TILES):
        lanes = slice(128 * i, 128 * (i + 1))
        rl[pl.ds(i, MODES, stride=8), :] = res_ref[:, lanes] * jnp.sqrt(rate_ref[:, lanes])
    for j in range(4):
        mix(0, j)

    rate = rate_ref[:, tile(p, 128)]
    step_w = jnp.exp(-float(ROWS) * rate)
    layer_w = jnp.exp(-float(ROWS * PLANE) * rate)
    blank = jnp.zeros((MODES, 128), F32)
    arrive(h_in)
    state = blank
    for b in range(PLANE):
        so[b * 16 : (b + 1) * 16, :] = state
        state = step_w * state + hin[b * 16 : (b + 1) * 16, :]
    yin[tile(y, 16), :] = state
    y_in = to_layers(yin, 16)
    g_sib.wait_recv()
    for j in range(4):
        mix(1, j)
    arrive(y_in)
    before = blank
    for b in range(LAYERS):
        before = jnp.where(b < y, layer_w * before + yin[b * 16 : (b + 1) * 16, :], before)
    for b in range(PLANE):
        so[b * 16 : (b + 1) * 16, :] += before
        before = step_w * before
    s_in = to_owners(so, sin, 16)
    far_part(2)
    far_part(3)
    far_pass(1)

    loads["q"].wait()
    arrive(s_in)

    def forward(t, h):
        for u in range(2):
            at_row = t * 2 + u
            x = xs[rows8(at_row), :]
            h = tuple(decay(m) * h[m] + x for m in range(MODES))
            for m in range(MODES):
                hb[rows8(at_row * MODES + m), :] = h[m]
            ys[rows8(at_row), :] = tree([amplitude(m) * h[m] for m in range(MODES)])
        return h

    lax.fori_loop(
        0, ROWS // 2, forward,
        tuple(sin[pl.ds(m, TILES, stride=MODES), :] for m in range(MODES)),
    )

    gat_slot = ids(CHUNKS * (PLANE - 1))
    other = place(0, 1)
    theirs = tile(other, ROWS)
    distant = tile(place(2, 0), ROWS)
    gat_z, gat_x2, gat_in = [], [], []

    def spread(chunk):
        slot = gat_slot + chunk * (PLANE - 1)
        block = gat[chunk].at[mine]
        gat_z.append(send(block, block, (y * PLANE + other, c), slot))
        gat_x2.append(send(block, block, across(2), slot + 2))
        gat_in.append([send(block, block, across(k), slot + k) for k in (1, 3)])

    def spread_more(chunk):
        slot = gat_slot + chunk * (PLANE - 1) + 4
        block = gat[chunk].at[theirs]
        gat_z[chunk].wait_recv()
        gat_in[chunk] += [send(block, block, across(k), slot + k // 2) for k in (1, 3)]
        if chunk in straight:
            gat_in[chunk] += [gat_x2[chunk], send(block, block, across(2), slot + 2)]
            return
        block = gat[chunk].at[distant]
        gat_x2[chunk].wait_recv()
        gat_in[chunk].append(send(block, block, (y * PLANE + other, c), slot + 2))

    straight = (0,)
    starts = [sum(WIDTHS[:n]) for n in range(CHUNKS)]
    for i in range(TILES):
        lanes = slice(128 * i, 128 * (i + 1))
        out = ys[pl.ds(i, ROWS, stride=8), :].astype(BF16)
        co[:, lanes] = out
        gated = (q_ref[:, lanes].astype(F32) * out.astype(F32)).astype(BF16)
        chunk = max(n for n in range(CHUNKS) if starts[n] <= 128 * i)
        from_lane = 128 * i - starts[chunk]
        gat[chunk][mine, from_lane : from_lane + 128] = gated
        if 128 * (i + 1) == WIDTHS[0]:
            spread(0)

    far_part(0)
    far_pass(2)
    g_pass[1].wait_recv()
    mix(3, 1)
    far_pass(3)
    spread(1)
    g_pass[2].wait_recv()
    mix(3, 2)
    arrive(a_near)
    a_sib = [send(at.at[c], at.at[c], (s, sib), a_slot + 14)]
    spread_more(0)
    g_pass[3].wait_recv()
    mix(3, 3)
    far_pass(0)
    arrive(a_cross)
    a_sib.append(send(at.at[far], at.at[far], (s, sib), a_slot + 15))
    g_pass[0].wait_recv()
    mix(3, 0)
    for i in range(TILES):
        lanes = slice(128 * i, 128 * (i + 1))
        mixed = gm[:, lanes].astype(BF16).astype(F32)
        gq_ref[:, lanes] = (mixed * co[:, lanes].astype(F32)).astype(BF16)
        cot = (mixed * q_ref[:, lanes].astype(F32)).astype(BF16)
        cs[pl.ds(i, ROWS, stride=8), :] = cot.astype(F32)

    def behind(n, g):
        for u in range(4):
            cot = cs[rows8(ROWS - 1 - (n * 4 + u)), :]
            g = tuple(decay(m) * g[m] + cot for m in range(MODES))
        return g

    g = lax.fori_loop(0, ROWS // 4, behind, (zero,) * MODES)
    for m in range(MODES):
        gs[pl.ds(m, TILES, stride=MODES), :] = g[m]
    g_in = to_owners(gs, gin, 16)
    spread(2)
    spread_more(1)
    spread(3)

    half = MODES // 2
    for part in range(2):
        modes = range(part * half, (part + 1) * half)

        def backward(n, carry, modes=modes):
            g, plain, ramp = carry
            for u in range(2):
                at_row = ROWS - 1 - (n * 2 + u)
                cot = cs[rows8(at_row), :]
                states = [hb[rows8(at_row * MODES + m), :] for m in modes]
                g = tuple(decay(m) * g[j] + cot for j, m in enumerate(modes))
                plain = tuple(plain[j] + states[j] * cot for j in range(half))
                ramp = tuple(ramp[j] + states[j] * g[j] for j in range(half))
            return g, plain, ramp

        found = lax.fori_loop(0, ROWS // 2, backward, ((zero,) * half,) * 3)
        for j, m in enumerate(modes):
            for n in range(2):
                pq[pl.ds(n * 16 + m, TILES, stride=48), :] = found[n + 1][j]

    rs_slot = ids(CHUNKS * 3)
    relay_slot = ids(RELAYED * 2)
    rs_in, relay_in = [], []
    top, low = pl.ds(0, PIECE // 2), pl.ds(PIECE // 2, PIECE // 2)

    def partial(chunk, k):
        return jnp.dot(at[(y + k) % LAYERS], gat[chunk][...], preferred_element_type=F32)

    def product(chunk):
        arrive(gat_in[chunk])
        slot = rs_slot + chunk * 3
        value = partial(chunk, 2).astype(BF16)
        if chunk < RELAYED:
            relay_send[chunk][...] = value
            relay_in.append([
                send(relay_send[chunk].at[rows], relay_recv[chunk].at[rows], layer(k),
                     relay_slot + chunk * 2 + n)
                for n, (rows, k) in enumerate(((top, 1), (low, 3)))
            ])
            for n, k in enumerate((1, 3)):
                held[chunk][n] = partial(chunk, k)
        else:
            for n, k in ((2, 2), (0, 1), (1, 3)):
                rs_send[chunk][n] = value if k == 2 else partial(chunk, k).astype(BF16)
                rs_in.append(
                    send(rs_send[chunk].at[n], rs_recv[chunk].at[n], layer(k), slot + n)
                )
        own[:, starts[chunk] : starts[chunk] + WIDTHS[chunk]] = partial(chunk, 0)

    def pass_on(chunk):
        arrive(relay_in[chunk])
        for n, (k, added, alone) in enumerate(((1, top, low), (3, low, top))):
            value = held[chunk][n, added, :] + relay_recv[chunk][added, :].astype(F32)
            rs_send[chunk][n, added, :] = value.astype(BF16)
            rs_send[chunk][n, alone, :] = held[chunk][n, alone, :].astype(BF16)
            rs_in.append(
                send(rs_send[chunk].at[n], rs_recv[chunk].at[n], layer(k), rs_slot + chunk * 3 + n)
            )

    arrive(a_sib)
    product(0)
    spread_more(2)
    spread(4)

    arrive(g_in)
    state = blank
    for b in reversed(range(PLANE)):
        to[b * 16 : b * 16 + 16, :] = state
        state = step_w * state + gin[b * 16 : b * 16 + 16, :]
    yin2[tile(y, 16), :] = state
    y2_in = to_layers(yin2, 16)

    def reach(t, z):
        for u in range(2):
            z = tuple(
                decay(m) * (z[m] + hb[rows8((t * 2 + u) * MODES + m), :]) for m in range(MODES)
            )
        return z

    z = lax.fori_loop(0, ROWS // 2, reach, (zero,) * MODES)
    for m in range(MODES):
        pq[pl.ds(32 + m, TILES, stride=48), :] = z[m]

    pass_on(0)
    product(1)
    spread_more(3)

    arrive(y2_in)
    after, chosen = blank, blank
    for b in reversed(range(LAYERS)):
        chosen = jnp.where(b == y, after, chosen)
        after = layer_w * after + yin2[b * 16 : b * 16 + 16, :]
    for b in reversed(range(PLANE)):
        to[b * 16 : b * 16 + 16, :] += chosen
        chosen = step_w * chosen
    t_in = to_owners(to, tin, 16)
    p_in = to_owners(pq, pin, 48)
    pass_on(1)
    product(2)
    spread_more(4)

    arrive(p_in)
    plain, ramp = blank, blank
    for b in range(PLANE):
        p_b, q_b, z_b = (pin[b * 48 + n * 16 : b * 48 + (n + 1) * 16, :] for n in range(3))
        plain = plain + p_b
        ramp = ramp + q_b + to[b * 16 : b * 16 + 16, :] * z_b
    yp[pl.ds(pl.multiple_of(y * 32, 16), 16), :] = plain
    yp[pl.ds(pl.multiple_of(y * 32 + 16, 16), 16), :] = ramp
    yp_in = to_layers(yp, 32)

    arrive(t_in)

    def final(n, g):
        for u in range(2):
            at_row = ROWS - 1 - (n * 2 + u)
            cot = cs[rows8(at_row), :]
            g = tuple(decay(m) * g[m] + cot for m in range(MODES))
            ys[rows8(at_row), :] = tree([amplitude(m) * g[m] for m in range(MODES)])
        return g

    lax.fori_loop(
        0, ROWS // 2, final,
        tuple(tin[pl.ds(m, TILES, stride=MODES), :] for m in range(MODES)),
    )
    for i in range(TILES):
        lanes = slice(128 * i, 128 * (i + 1))
        back = ys[pl.ds(i, ROWS, stride=8), :].astype(BF16).astype(F32)
        gk_ref[:, lanes] = (back * v_ref[:, lanes].astype(F32)).astype(BF16)
        gv_ref[:, lanes] = (back * k_ref[:, lanes].astype(F32)).astype(BF16)

    pass_on(2)
    product(3)
    product(4)

    arrive(yp_in)
    plain, ramp = blank, blank
    for b in range(LAYERS):
        plain = plain + yp[b * 32 : b * 32 + 16, :]
        ramp = ramp + yp[b * 32 + 16 : b * 32 + 32, :]
    root = jnp.sqrt(rate) * grad_scale
    pr[0:16, :] = root * plain
    pr[16:32, :] = res_ref[:, tile(p, 128)] * root * (0.5 * plain - rate * (ramp - plain))
    slot = ids(PLANE - 1)
    pr_in = [send(pr, prin.at[tile(p, 32)], plane(k), slot + k - 1) for k in range(1, PLANE)]
    prin[tile(p, 32), :] = pr[...]

    arrive(pr_in)
    for i in range(TILES):
        lanes = slice(128 * i, 128 * (i + 1))
        gr_ref[:, lanes] = prin[i * 32 : i * 32 + 16, :]
        gl_ref[:, lanes] = prin[i * 32 + 16 : i * 32 + 32, :]
    arrive(rs_in)
    for chunk in range(CHUNKS):
        cols = slice(starts[chunk], starts[chunk] + WIDTHS[chunk])
        total = own[:, cols]
        for k in range(2 if chunk < RELAYED else 3):
            total = total + rs_recv[chunk][k].astype(F32)
        gw_ref[:, cols] = total * grad_scale
    for copy in sends:
        copy.wait_send()


SLOTS = 160


def settle(*refs):
    count = len(refs) // 2
    for n in range(count):
        refs[count + n][...] = refs[n][...]


def per_device(query_act, key_act, value_act, residue, decay_rate, out_weight, grad_out):
    vmem = pl.BlockSpec(memory_space=pltpu.VMEM)
    shape = jax.ShapeDtypeStruct
    small = shape((ROWS, COLS), BF16)
    modal = shape((MODES, COLS), F32)
    scratch = [
        ((ROWS, COLS), BF16),
        ((ROWS, COLS), BF16),
        ((ROWS, COLS), BF16),
        ((ROWS, DPART), BF16),
        ((MODES, COLS), F32),
        ((MODES, COLS), F32),
        ((PARTS * DPART, COLS), BF16),
        ((ROWS * 8, 128), F32),
        ((ROWS * 8, 128), F32),
        ((ROWS * 8, 128), F32),
        ((ROWS * MODES * 8, 128), F32),
        ((MODES * 8, 128), F32),
        ((MODES * 8, 128), F32),
        ((PARTS, ROWS, DPART), BF16),
        ((PLANE, PIECE, ROWS), BF16),
        ((4, PIECE, ROWS), BF16),
        ((PARTS, PIECE, PLANE * ROWS), BF16),
        [((PLANE * ROWS, wide), BF16) for wide in WIDTHS],
        ((ROWS, COLS), F32),
        ((ROWS, COLS), BF16),
        ((TILES * 16, 128), F32),
        ((PLANE * 16, 128), F32),
        ((PLANE * 16, 128), F32),
        ((TILES * 16, 128), F32),
        ((LAYERS * 16, 128), F32),
        ((TILES * 16, 128), F32),
        ((PLANE * 16, 128), F32),
        ((LAYERS * 16, 128), F32),
        ((PLANE * 16, 128), F32),
        ((TILES * 16, 128), F32),
        ((TILES * 48, 128), F32),
        ((PLANE * 48, 128), F32),
        ((LAYERS * 32, 128), F32),
        ((32, 128), F32),
        ((TILES * 32, 128), F32),
        [((3, PIECE, wide), BF16) for wide in WIDTHS],
        [((3, PIECE, wide), BF16) for wide in WIDTHS],
        [((PIECE, wide), BF16) for wide in WIDTHS[:RELAYED]],
        [((PIECE, wide), BF16) for wide in WIDTHS[:RELAYED]],
        [((2, PIECE, wide), F32) for wide in WIDTHS[:RELAYED]],
        ((PIECE, COLS), F32),
    ]
    outs = (small, small, small, shape((PIECE, COLS), F32), modal, modal)
    found = pl.pallas_call(
        body,
        out_shape=outs,
        in_specs=[pl.BlockSpec(memory_space=pl.ANY)] * 7,
        out_specs=(vmem,) * 6,
        scratch_shapes=[
            [pltpu.VMEM(*one) for one in entry] if isinstance(entry, list) else pltpu.VMEM(*entry)
            for entry in scratch
        ]
        + [
            pltpu.SemaphoreType.DMA((10,)),
            pltpu.SemaphoreType.DMA((SLOTS,)),
            pltpu.SemaphoreType.DMA((SLOTS,)),
        ],
        compiler_params=pltpu.CompilerParams(
            collective_id=0, has_side_effects=True, vmem_limit_bytes=56 * 2**20
        ),
        cost_estimate=pl.CostEstimate(
            flops=2 * 2**31, bytes_accessed=20 * 2**20, transcendentals=0
        ),
    )(query_act, key_act, value_act, grad_out, residue, decay_rate, out_weight)
    return pl.pallas_call(
        settle,
        out_shape=outs,
        in_specs=[vmem] * len(outs),
        out_specs=(vmem,) * len(outs),
    )(*found)


def solution(mesh):
    both = P("seq", "chan")
    chan = P(None, "chan")
    return jax.shard_map(
        per_device,
        mesh=mesh,
        in_specs=(both, both, both, chan, chan, chan, both),
        out_specs=(both, both, both, both, chan, chan),
        check_vma=False,
    )
```

```python
import jax
import jax.numpy as jnp
from jax import lax
from jax.experimental import pallas as pl
from jax.experimental.pallas import tpu as pltpu
from jax.sharding import PartitionSpec as P

MESH = pl.DeviceIdType.MESH
F32 = jnp.float32
BF16 = jnp.bfloat16
ROWS = 128
COLS = 1024
TILES = 8
MODES = 16
PLANE = 8
LAYERS = 4
PARTS = 4
DPART = 2048
PIECE = 256
WIDTHS = (128, 128, 128, 128, 128, 128, 128, 128)
GROUPS = ((0, 1), (2, 3), (4, 5), (6,), (7,))
CHUNKS = len(WIDTHS)
RELAYED = 6
DEPTH = 512


def rows8(index):
    return pl.ds(pl.multiple_of(index * 8, 8), 8)


def body(
    q_hbm, k_hbm, v_hbm, g_hbm, res_hbm, rate_hbm, w_ref,
    gq_ref, gk_ref, gv_ref, gw_ref, gr_ref, gl_ref,
    q_ref, k_ref, v_ref, g_ref, res_ref, rate_ref,
    wv, xs, cs, ys, hb, al, rl, gall, gt, zbuf, turned, at, gat, gm, co,
    hs, hin, so, sin, yin, gs, gin, yin2, to, tin, pq, pin, yp, pr, prin,
    rs_send, rs_recv, relay_send, relay_recv, held, own, wsem, ssem, rsem,
):
    s = lax.axis_index("seq")
    c = lax.axis_index("chan")
    y = s // PLANE
    p = s % PLANE
    sib = (c // 2) * 2 + (1 - c % 2)
    far = (c + 2) % PARTS
    farsib = (sib + 2) % PARTS
    grad_scale = float(ROWS * PLANE * LAYERS) ** -0.5
    counter = [0]
    sends = []

    def plane(k):
        return (y * PLANE + (p + k) % PLANE, c)

    def across(k):
        return (y * PLANE + (p + 2 * k) % PLANE, c)

    def place(x_step, z_turn):
        return ((p // 2 + x_step) % 4) * 2 + (p % 2 + z_turn) % 2

    def layer(k):
        return (((y + k) % LAYERS) * PLANE + p, c)

    def ids(count):
        counter[0] += count
        assert counter[0] <= SLOTS
        return counter[0] - count

    def send(src, dst, device, slot):
        copy = pltpu.make_async_remote_copy(
            src_ref=src, dst_ref=dst, send_sem=ssem.at[slot], recv_sem=rsem.at[slot],
            device_id=device, device_id_type=MESH,
        )
        copy.start()
        sends.append(copy)
        return copy

    def tile(index, size):
        return pl.ds(pl.multiple_of(index * size, size), size)

    def decay(m):
        return al[m * 8 : (m + 1) * 8, :]

    def amplitude(m):
        return rl[m * 8 : (m + 1) * 8, :]

    def tree(terms):
        while len(terms) > 1:
            terms = [terms[n] + terms[n + 1] for n in range(0, len(terms), 2)]
        return terms[0]

    barrier = pltpu.get_barrier_semaphore()
    greeted = [plane(k) for k in range(1, PLANE)] + [layer(k) for k in range(1, LAYERS)]
    greeted += [(s, sib), (s, far)]
    beside = y * PLANE + place(0, 1)
    greeted.append((beside, far))
    for device in greeted:
        pl.semaphore_signal(barrier, inc=1, device_id=device, device_id_type=MESH)

    loads = {}
    for n, (name, src, dst) in enumerate((
        ("rate", rate_hbm, rate_ref), ("k", k_hbm, k_ref), ("v", v_hbm, v_ref),
        ("res", res_hbm, res_ref), ("g", g_hbm, g_ref), ("q", q_hbm, q_ref),
    )):
        loads[name] = pltpu.make_async_copy(src, dst, wsem.at[PARTS + n])
        loads[name].start()
    order = (c, sib, far, farsib)
    wcopies = []
    for n, h in enumerate(order):
        part = tile(h, DPART)
        copy = pltpu.make_async_copy(w_ref.at[part], wv.at[part], wsem.at[n])
        copy.start()
        wcopies.append(copy)

    for name in ("rate", "k", "v"):
        loads[name].wait()
    for i in range(TILES):
        lanes = slice(128 * i, 128 * (i + 1))
        al[pl.ds(i, MODES, stride=8), :] = jnp.exp(-rate_ref[:, lanes])
        x = (k_ref[:, lanes].astype(F32) * v_ref[:, lanes].astype(F32)).astype(BF16)
        xs[pl.ds(i, ROWS, stride=8), :] = x.astype(F32)

    zero = jnp.zeros((8, 128), F32)

    def ahead(t, h):
        for u in range(4):
            x = xs[rows8(t * 4 + u), :]
            h = tuple(decay(m) * h[m] + x for m in range(MODES))
        return h

    h = lax.fori_loop(0, ROWS // 4, ahead, (zero,) * MODES)
    for m in range(MODES):
        hs[pl.ds(m, TILES, stride=MODES), :] = h[m]

    pl.semaphore_wait(barrier, len(greeted))

    def to_owners(src, dst, size):
        slot = ids(PLANE - 1)
        copies = [
            send(src.at[tile((p + k) % PLANE, size)], dst.at[tile(p, size)], plane(k), slot + k - 1)
            for k in range(1, PLANE)
        ]
        dst[tile(p, size), :] = src[tile(p, size), :]
        return copies

    def to_layers(ref, size):
        slot = ids(LAYERS - 1)
        block = ref.at[tile(y, size)]
        return [send(block, block, layer(k), slot + k - 1) for k in range(1, LAYERS)]

    def arrive(copies):
        for copy in copies:
            copy.wait_recv()

    h_in = to_owners(hs, hin, 16)
    loads["g"].wait()
    g_slot = ids(9)
    g_sib = send(g_ref, gall.at[c], (s, sib), g_slot)

    def far_cols(n):
        return tile((p // 2 + n) % 4, DEPTH)

    def far_part(n):
        cols = far_cols(n)
        g_far[n] = send(g_ref.at[:, cols], gall.at[c, :, cols], (s, far), g_slot + 1 + n)

    def far_pass(n):
        cols = far_cols(n)
        g_far[n].wait_recv()
        block = gall.at[far, :, cols]
        g_pass[n] = send(block, block, (s, sib), g_slot + 5 + n)
        turned[n] = gall[far, :, tile(place(n, 0), PIECE)].T
        if n == 0:
            at[far, :, mine] = turned[0]
        else:
            a_cross.append(
                send(turned.at[n], at.at[far, :, mine], across(n), a_slot + 10 + n)
            )
        mix(2, n)

    g_far, g_pass = {}, {}
    gall[c] = g_ref[...]

    for turn in range(2):
        for k in range(4):
            gt[turn, k] = g_ref[:, tile(place(k, turn), PIECE)].T
    a_slot = ids(16)
    mine = tile(p, ROWS)
    z_in = [send(gt.at[1], zbuf.at[0], (beside, c), a_slot + 3)]
    z_in.append(send(gt.at[1], zbuf.at[1], (beside, far), a_slot + 7))
    a_near = [
        send(gt.at[0, k], at.at[c, :, mine], across(k), a_slot + k - 1) for k in range(1, 4)
    ]
    at[c, :, mine] = gt[0, 0]
    a_cross = []
    far_part(1)

    seen = set()

    def mix(n, j):
        h = order[n]
        if n not in seen:
            seen.add(n)
            wcopies[n].wait()
        if n >= 2:
            j = (p // 2 + j) % 4
        deep = pl.ds(pl.multiple_of(h * DPART + j * DEPTH, DEPTH), DEPTH)
        cols = tile(j, DEPTH)
        gm[...] += jnp.dot(gall[h, :, cols], wv[deep, :], preferred_element_type=F32)

    gm[...] = jnp.zeros_like(gm)
    loads["res"].wait()
    for i in range(TILES):
        lanes = slice(128 * i, 128 * (i + 1))
        rl[pl.ds(i, MODES, stride=8), :] = res_ref[:, lanes] * jnp.sqrt(rate_ref[:, lanes])
    for j in range(4):
        mix(0, j)

    rate = rate_ref[:, tile(p, 128)]
    step_w = jnp.exp(-float(ROWS) * rate)
    layer_w = jnp.exp(-float(ROWS * PLANE) * rate)
    blank = jnp.zeros((MODES, 128), F32)
    arrive(h_in)
    state = blank
    for b in range(PLANE):
        so[b * 16 : (b + 1) * 16, :] = state
        state = step_w * state + hin[b * 16 : (b + 1) * 16, :]
    yin[tile(y, 16), :] = state
    y_in = to_layers(yin, 16)
    g_sib.wait_recv()
    for j in range(4):
        mix(1, j)
    arrive(y_in)
    before = blank
    for b in range(LAYERS):
        before = jnp.where(b < y, layer_w * before + yin[b * 16 : (b + 1) * 16, :], before)
    for b in range(PLANE):
        so[b * 16 : (b + 1) * 16, :] += before
        before = step_w * before
    s_in = to_owners(so, sin, 16)
    far_part(2)
    far_part(3)
    beyond = tile(place(0, 1), ROWS)
    for n, (h, found) in enumerate(((c, a_near), (far, a_cross))):
        z_in[n].wait_recv()
        at[h, :, beyond] = zbuf[n, 0]
        found += [
            send(zbuf.at[n, k], at.at[h, :, beyond], across(k), a_slot + 3 + 4 * n + k)
            for k in range(1, 4)
        ]
    far_pass(1)

    loads["q"].wait()
    arrive(s_in)

    def forward(t, h):
        for u in range(2):
            at_row = t * 2 + u
            x = xs[rows8(at_row), :]
            h = tuple(decay(m) * h[m] + x for m in range(MODES))
            for m in range(MODES):
                hb[rows8(at_row * MODES + m), :] = h[m]
            ys[rows8(at_row), :] = tree([amplitude(m) * h[m] for m in range(MODES)])
        return h

    lax.fori_loop(
        0, ROWS // 2, forward,
        tuple(sin[pl.ds(m, TILES, stride=MODES), :] for m in range(MODES)),
    )

    gat_slot = ids(CHUNKS * (PLANE - 1))
    other = place(0, 1)
    theirs = tile(other, ROWS)
    distant = tile(place(2, 0), ROWS)
    gat_z, gat_x2, gat_in = [], [], []

    def spread(group):
        for chunk in GROUPS[group]:
            spread_one(chunk)

    def spread_one(chunk):
        slot = gat_slot + chunk * (PLANE - 1)
        block = gat[chunk].at[mine]
        gat_z.append(send(block, block, (y * PLANE + other, c), slot))
        gat_x2.append(send(block, block, across(2), slot + 2))
        gat_in.append([send(block, block, across(k), slot + k) for k in (1, 3)])

    def spread_more(group):
        for chunk in GROUPS[group]:
            spread_more_one(chunk)

    def spread_more_one(chunk):
        slot = gat_slot + chunk * (PLANE - 1) + 4
        block = gat[chunk].at[theirs]
        gat_z[chunk].wait_recv()
        gat_in[chunk] += [send(block, block, across(k), slot + k // 2) for k in (1, 3)]
        if chunk in straight:
            gat_in[chunk] += [gat_x2[chunk], send(block, block, across(2), slot + 2)]
            return
        block = gat[chunk].at[distant]
        gat_x2[chunk].wait_recv()
        gat_in[chunk].append(send(block, block, (y * PLANE + other, c), slot + 2))

    straight = GROUPS[0]
    starts = [sum(WIDTHS[:n]) for n in range(CHUNKS)]
    for i in range(TILES):
        lanes = slice(128 * i, 128 * (i + 1))
        out = ys[pl.ds(i, ROWS, stride=8), :].astype(BF16)
        co[:, lanes] = out
        gated = (q_ref[:, lanes].astype(F32) * out.astype(F32)).astype(BF16)
        chunk = max(n for n in range(CHUNKS) if starts[n] <= 128 * i)
        from_lane = 128 * i - starts[chunk]
        gat[chunk][mine, from_lane : from_lane + 128] = gated
        if 128 * (i + 1) == sum(WIDTHS[n] for n in GROUPS[0]):
            spread(0)

    far_part(0)
    far_pass(2)
    g_pass[1].wait_recv()
    mix(3, 1)
    far_pass(3)
    spread(1)
    g_pass[2].wait_recv()
    mix(3, 2)
    arrive(a_near)
    a_sib = [send(at.at[c], at.at[c], (s, sib), a_slot + 14)]
    spread_more(0)
    g_pass[3].wait_recv()
    mix(3, 3)
    far_pass(0)
    arrive(a_cross)
    a_sib.append(send(at.at[far], at.at[far], (s, sib), a_slot + 15))
    g_pass[0].wait_recv()
    mix(3, 0)
    for i in range(TILES):
        lanes = slice(128 * i, 128 * (i + 1))
        mixed = gm[:, lanes].astype(BF16).astype(F32)
        gq_ref[:, lanes] = (mixed * co[:, lanes].astype(F32)).astype(BF16)
        cot = (mixed * q_ref[:, lanes].astype(F32)).astype(BF16)
        cs[pl.ds(i, ROWS, stride=8), :] = cot.astype(F32)

    def behind(n, g):
        for u in range(4):
            cot = cs[rows8(ROWS - 1 - (n * 4 + u)), :]
            g = tuple(decay(m) * g[m] + cot for m in range(MODES))
        return g

    g = lax.fori_loop(0, ROWS // 4, behind, (zero,) * MODES)
    for m in range(MODES):
        gs[pl.ds(m, TILES, stride=MODES), :] = g[m]
    g_in = to_owners(gs, gin, 16)
    spread(2)
    spread_more(1)
    spread(3)

    half = MODES // 2
    for part in range(2):
        modes = range(part * half, (part + 1) * half)

        def backward(n, carry, modes=modes):
            g, plain, ramp = carry
            for u in range(2):
                at_row = ROWS - 1 - (n * 2 + u)
                cot = cs[rows8(at_row), :]
                states = [hb[rows8(at_row * MODES + m), :] for m in modes]
                g = tuple(decay(m) * g[j] + cot for j, m in enumerate(modes))
                plain = tuple(plain[j] + states[j] * cot for j in range(half))
                ramp = tuple(ramp[j] + states[j] * g[j] for j in range(half))
            return g, plain, ramp

        found = lax.fori_loop(0, ROWS // 2, backward, ((zero,) * half,) * 3)
        for j, m in enumerate(modes):
            for n in range(2):
                pq[pl.ds(n * 16 + m, TILES, stride=48), :] = found[n + 1][j]

    rs_slot = ids(CHUNKS * 3)
    relay_slot = ids(RELAYED * 2)
    rs_in, relay_in = [], []
    top, low = pl.ds(0, PIECE // 2), pl.ds(PIECE // 2, PIECE // 2)

    def partial(chunk, k):
        return jnp.dot(at[(y + k) % LAYERS], gat[chunk][...], preferred_element_type=F32)

    def product(group):
        for chunk in GROUPS[group]:
            product_one(chunk)

    def product_one(chunk):
        arrive(gat_in[chunk])
        slot = rs_slot + chunk * 3
        value = partial(chunk, 2).astype(BF16)
        if chunk < RELAYED:
            relay_send[chunk][...] = value
            relay_in.append([
                send(relay_send[chunk].at[rows], relay_recv[chunk].at[rows], layer(k),
                     relay_slot + chunk * 2 + n)
                for n, (rows, k) in enumerate(((top, 1), (low, 3)))
            ])
            for n, k in enumerate((1, 3)):
                held[chunk][n] = partial(chunk, k)
        else:
            for n, k in ((2, 2), (0, 1), (1, 3)):
                rs_send[chunk][n] = value if k == 2 else partial(chunk, k).astype(BF16)
                rs_in.append(
                    send(rs_send[chunk].at[n], rs_recv[chunk].at[n], layer(k), slot + n)
                )
        own[:, starts[chunk] : starts[chunk] + WIDTHS[chunk]] = partial(chunk, 0)

    def pass_on(group):
        for chunk in GROUPS[group]:
            pass_on_one(chunk)

    def pass_on_one(chunk):
        arrive(relay_in[chunk])
        for n, (k, added, alone) in enumerate(((1, top, low), (3, low, top))):
            value = held[chunk][n, added, :] + relay_recv[chunk][added, :].astype(F32)
            rs_send[chunk][n, added, :] = value.astype(BF16)
            rs_send[chunk][n, alone, :] = held[chunk][n, alone, :].astype(BF16)
            rs_in.append(
                send(rs_send[chunk].at[n], rs_recv[chunk].at[n], layer(k), rs_slot + chunk * 3 + n)
            )

    arrive(a_sib)
    product(0)
    spread_more(2)
    spread(4)

    arrive(g_in)
    state = blank
    for b in reversed(range(PLANE)):
        to[b * 16 : b * 16 + 16, :] = state
        state = step_w * state + gin[b * 16 : b * 16 + 16, :]
    yin2[tile(y, 16), :] = state
    y2_in = to_layers(yin2, 16)

    def reach(t, z):
        for u in range(2):
            z = tuple(
                decay(m) * (z[m] + hb[rows8((t * 2 + u) * MODES + m), :]) for m in range(MODES)
            )
        return z

    z = lax.fori_loop(0, ROWS // 2, reach, (zero,) * MODES)
    for m in range(MODES):
        pq[pl.ds(32 + m, TILES, stride=48), :] = z[m]

    pass_on(0)
    product(1)
    spread_more(3)

    arrive(y2_in)
    after, chosen = blank, blank
    for b in reversed(range(LAYERS)):
        chosen = jnp.where(b == y, after, chosen)
        after = layer_w * after + yin2[b * 16 : b * 16 + 16, :]
    for b in reversed(range(PLANE)):
        to[b * 16 : b * 16 + 16, :] += chosen
        chosen = step_w * chosen
    t_in = to_owners(to, tin, 16)
    p_in = to_owners(pq, pin, 48)
    pass_on(1)
    product(2)
    spread_more(4)

    arrive(p_in)
    plain, ramp = blank, blank
    for b in range(PLANE):
        p_b, q_b, z_b = (pin[b * 48 + n * 16 : b * 48 + (n + 1) * 16, :] for n in range(3))
        plain = plain + p_b
        ramp = ramp + q_b + to[b * 16 : b * 16 + 16, :] * z_b
    yp[pl.ds(pl.multiple_of(y * 32, 16), 16), :] = plain
    yp[pl.ds(pl.multiple_of(y * 32 + 16, 16), 16), :] = ramp
    yp_in = to_layers(yp, 32)

    arrive(t_in)

    def final(n, g):
        for u in range(2):
            at_row = ROWS - 1 - (n * 2 + u)
            cot = cs[rows8(at_row), :]
            g = tuple(decay(m) * g[m] + cot for m in range(MODES))
            ys[rows8(at_row), :] = tree([amplitude(m) * g[m] for m in range(MODES)])
        return g

    lax.fori_loop(
        0, ROWS // 2, final,
        tuple(tin[pl.ds(m, TILES, stride=MODES), :] for m in range(MODES)),
    )
    for i in range(TILES):
        lanes = slice(128 * i, 128 * (i + 1))
        back = ys[pl.ds(i, ROWS, stride=8), :].astype(BF16).astype(F32)
        gk_ref[:, lanes] = (back * v_ref[:, lanes].astype(F32)).astype(BF16)
        gv_ref[:, lanes] = (back * k_ref[:, lanes].astype(F32)).astype(BF16)

    pass_on(2)
    product(3)
    product(4)

    arrive(yp_in)
    plain, ramp = blank, blank
    for b in range(LAYERS):
        plain = plain + yp[b * 32 : b * 32 + 16, :]
        ramp = ramp + yp[b * 32 + 16 : b * 32 + 32, :]
    root = jnp.sqrt(rate) * grad_scale
    pr[0:16, :] = root * plain
    pr[16:32, :] = res_ref[:, tile(p, 128)] * root * (0.5 * plain - rate * (ramp - plain))
    slot = ids(PLANE - 1)
    pr_in = [send(pr, prin.at[tile(p, 32)], plane(k), slot + k - 1) for k in range(1, PLANE)]
    prin[tile(p, 32), :] = pr[...]

    arrive(pr_in)
    for i in range(TILES):
        lanes = slice(128 * i, 128 * (i + 1))
        gr_ref[:, lanes] = prin[i * 32 : i * 32 + 16, :]
        gl_ref[:, lanes] = prin[i * 32 + 16 : i * 32 + 32, :]
    arrive(rs_in)
    for chunk in range(CHUNKS):
        cols = slice(starts[chunk], starts[chunk] + WIDTHS[chunk])
        total = own[:, cols]
        for k in range(2 if chunk < RELAYED else 3):
            total = total + rs_recv[chunk][k].astype(F32)
        gw_ref[:, cols] = total * grad_scale
    for copy in sends:
        copy.wait_send()


SLOTS = 192


def settle(*refs):
    count = len(refs) // 2
    for n in range(count):
        refs[count + n][...] = refs[n][...]


def per_device(query_act, key_act, value_act, residue, decay_rate, out_weight, grad_out):
    vmem = pl.BlockSpec(memory_space=pltpu.VMEM)
    shape = jax.ShapeDtypeStruct
    small = shape((ROWS, COLS), BF16)
    modal = shape((MODES, COLS), F32)
    scratch = [
        ((ROWS, COLS), BF16),
        ((ROWS, COLS), BF16),
        ((ROWS, COLS), BF16),
        ((ROWS, DPART), BF16),
        ((MODES, COLS), F32),
        ((MODES, COLS), F32),
        ((PARTS * DPART, COLS), BF16),
        ((ROWS * 8, 128), F32),
        ((ROWS * 8, 128), F32),
        ((ROWS * 8, 128), F32),
        ((ROWS * MODES * 8, 128), F32),
        ((MODES * 8, 128), F32),
        ((MODES * 8, 128), F32),
        ((PARTS, ROWS, DPART), BF16),
        ((2, 4, PIECE, ROWS), BF16),
        ((2, 4, PIECE, ROWS), BF16),
        ((4, PIECE, ROWS), BF16),
        ((PARTS, PIECE, PLANE * ROWS), BF16),
        [((PLANE * ROWS, wide), BF16) for wide in WIDTHS],
        ((ROWS, COLS), F32),
        ((ROWS, COLS), BF16),
        ((TILES * 16, 128), F32),
        ((PLANE * 16, 128), F32),
        ((PLANE * 16, 128), F32),
        ((TILES * 16, 128), F32),
        ((LAYERS * 16, 128), F32),
        ((TILES * 16, 128), F32),
        ((PLANE * 16, 128), F32),
        ((LAYERS * 16, 128), F32),
        ((PLANE * 16, 128), F32),
        ((TILES * 16, 128), F32),
        ((TILES * 48, 128), F32),
        ((PLANE * 48, 128), F32),
        ((LAYERS * 32, 128), F32),
        ((32, 128), F32),
        ((TILES * 32, 128), F32),
        [((3, PIECE, wide), BF16) for wide in WIDTHS],
        [((3, PIECE, wide), BF16) for wide in WIDTHS],
        [((PIECE, wide), BF16) for wide in WIDTHS[:RELAYED]],
        [((PIECE, wide), BF16) for wide in WIDTHS[:RELAYED]],
        [((2, PIECE, wide), F32) for wide in WIDTHS[:RELAYED]],
        ((PIECE, COLS), F32),
    ]
    outs = (small, small, small, shape((PIECE, COLS), F32), modal, modal)
    found = pl.pallas_call(
        body,
        out_shape=outs,
        in_specs=[pl.BlockSpec(memory_space=pl.ANY)] * 7,
        out_specs=(vmem,) * 6,
        scratch_shapes=[
            [pltpu.VMEM(*one) for one in entry] if isinstance(entry, list) else pltpu.VMEM(*entry)
            for entry in scratch
        ]
        + [
            pltpu.SemaphoreType.DMA((10,)),
            pltpu.SemaphoreType.DMA((SLOTS,)),
            pltpu.SemaphoreType.DMA((SLOTS,)),
        ],
        compiler_params=pltpu.CompilerParams(
            collective_id=0, has_side_effects=True, vmem_limit_bytes=56 * 2**20
        ),
        cost_estimate=pl.CostEstimate(
            flops=2 * 2**31, bytes_accessed=20 * 2**20, transcendentals=0
        ),
    )(query_act, key_act, value_act, grad_out, residue, decay_rate, out_weight)
    return pl.pallas_call(
        settle,
        out_shape=outs,
        in_specs=[vmem] * len(outs),
        out_specs=(vmem,) * len(outs),
    )(*found)


def solution(mesh):
    both = P("seq", "chan")
    chan = P(None, "chan")
    return jax.shard_map(
        per_device,
        mesh=mesh,
        in_specs=(both, both, both, chan, chan, chan, both),
        out_specs=(both, both, both, both, chan, chan),
        check_vma=False,
    )
```

```python
import jax
import jax.numpy as jnp
from jax import lax
from jax.experimental import pallas as pl
from jax.experimental.pallas import tpu as pltpu
from jax.sharding import PartitionSpec as P

MESH = pl.DeviceIdType.MESH
F32 = jnp.float32
BF16 = jnp.bfloat16
ROWS = 128
COLS = 1024
TILES = 8
MODES = 16
PLANE = 8
LAYERS = 4
PARTS = 4
DPART = 2048
PIECE = 256
WIDTHS = (128, 128, 128, 128, 128, 128, 128, 128)
GROUPS = ((0, 1), (2, 3), (4, 5), (6,), (7,))
CHUNKS = len(WIDTHS)
RELAYED = 6
DEPTH = 512


def rows8(index):
    return pl.ds(pl.multiple_of(index * 8, 8), 8)


def body(
    q_hbm, k_hbm, v_hbm, g_hbm, res_hbm, rate_hbm, w_ref,
    gq_ref, gk_ref, gv_ref, gw_ref, gr_ref, gl_ref,
    q_ref, k_ref, v_ref, g_ref, res_ref, rate_ref,
    wv, xs, cs, ys, hb, al, rl, gall, gt, zbuf, turned, at, gat, gm, co,
    hs, hin, so, sin, yin, gs, gin, yin2, to, tin, pq, pin, yp, pr, prin,
    rs_send, rs_recv, relay_send, relay_recv, held, own, wsem, ssem, rsem,
):
    s = lax.axis_index("seq")
    c = lax.axis_index("chan")
    y = s // PLANE
    p = s % PLANE
    sib = (c // 2) * 2 + (1 - c % 2)
    far = (c + 2) % PARTS
    farsib = (sib + 2) % PARTS
    grad_scale = float(ROWS * PLANE * LAYERS) ** -0.5
    counter = [0]
    sends = []

    def plane(k):
        return (y * PLANE + (p + k) % PLANE, c)

    def across(k):
        return (y * PLANE + (p + 2 * k) % PLANE, c)

    def place(x_step, z_turn):
        return ((p // 2 + x_step) % 4) * 2 + (p % 2 + z_turn) % 2

    def layer(k):
        return (((y + k) % LAYERS) * PLANE + p, c)

    def ids(count):
        counter[0] += count
        assert counter[0] <= SLOTS
        return counter[0] - count

    def send(src, dst, device, slot):
        copy = pltpu.make_async_remote_copy(
            src_ref=src, dst_ref=dst, send_sem=ssem.at[slot], recv_sem=rsem.at[slot],
            device_id=device, device_id_type=MESH,
        )
        copy.start()
        sends.append(copy)
        return copy

    def tile(index, size):
        return pl.ds(pl.multiple_of(index * size, size), size)

    def decay(m):
        return al[m * 8 : (m + 1) * 8, :]

    def amplitude(m):
        return rl[m * 8 : (m + 1) * 8, :]

    def tree(terms):
        while len(terms) > 1:
            terms = [terms[n] + terms[n + 1] for n in range(0, len(terms), 2)]
        return terms[0]

    barrier = pltpu.get_barrier_semaphore()
    greeted = [plane(k) for k in range(1, PLANE)] + [layer(k) for k in range(1, LAYERS)]
    greeted += [(s, sib), (s, far)]
    beside = y * PLANE + place(0, 1)
    greeted.append((beside, far))
    for device in greeted:
        pl.semaphore_signal(barrier, inc=1, device_id=device, device_id_type=MESH)

    loads = {}
    for n, (name, src, dst) in enumerate((
        ("rate", rate_hbm, rate_ref), ("k", k_hbm, k_ref), ("v", v_hbm, v_ref),
        ("res", res_hbm, res_ref), ("g", g_hbm, g_ref), ("q", q_hbm, q_ref),
    )):
        loads[name] = pltpu.make_async_copy(src, dst, wsem.at[PARTS + n])
        loads[name].start()
    order = (c, sib, far, farsib)
    wcopies = []
    for n, h in enumerate(order):
        part = tile(h, DPART)
        copy = pltpu.make_async_copy(w_ref.at[part], wv.at[part], wsem.at[n])
        copy.start()
        wcopies.append(copy)

    for name in ("rate", "k", "v"):
        loads[name].wait()
    for i in range(TILES):
        lanes = slice(128 * i, 128 * (i + 1))
        al[pl.ds(i, MODES, stride=8), :] = jnp.exp(-rate_ref[:, lanes])
        x = (k_ref[:, lanes].astype(F32) * v_ref[:, lanes].astype(F32)).astype(BF16)
        xs[pl.ds(i, ROWS, stride=8), :] = x.astype(F32)

    zero = jnp.zeros((8, 128), F32)

    def ahead(t, h):
        for u in range(4):
            x = xs[rows8(t * 4 + u), :]
            h = tuple(decay(m) * h[m] + x for m in range(MODES))
        return h

    h = lax.fori_loop(0, ROWS // 4, ahead, (zero,) * MODES)
    for m in range(MODES):
        hs[pl.ds(m, TILES, stride=MODES), :] = h[m]

    pl.semaphore_wait(barrier, len(greeted))

    def to_owners(src, dst, size):
        slot = ids(PLANE - 1)
        copies = [
            send(src.at[tile((p + k) % PLANE, size)], dst.at[tile(p, size)], plane(k), slot + k - 1)
            for k in range(1, PLANE)
        ]
        dst[tile(p, size), :] = src[tile(p, size), :]
        return copies

    def to_layers(ref, size):
        slot = ids(LAYERS - 1)
        block = ref.at[tile(y, size)]
        return [send(block, block, layer(k), slot + k - 1) for k in range(1, LAYERS)]

    def arrive(copies):
        for copy in copies:
            copy.wait_recv()

    h_in = to_owners(hs, hin, 16)
    loads["g"].wait()
    g_slot = ids(9)
    g_sib = send(g_ref, gall.at[c], (s, sib), g_slot)

    def far_cols(n):
        return tile((p // 2 + n) % 4, DEPTH)

    def far_part(n):
        cols = far_cols(n)
        g_far[n] = send(g_ref.at[:, cols], gall.at[c, :, cols], (s, far), g_slot + 1 + n)

    def far_pass(n):
        cols = far_cols(n)
        g_far[n].wait_recv()
        block = gall.at[far, :, cols]
        g_pass[n] = send(block, block, (s, sib), g_slot + 5 + n)
        turned[n] = gall[far, :, tile(place(n, 0), PIECE)].T
        if n == 0:
            at[far, :, mine] = turned[0]
        else:
            a_cross.append(
                send(turned.at[n], at.at[far, :, mine], across(n), a_slot + 10 + n)
            )
        mix(2, n)

    g_far, g_pass = {}, {}
    gall[c] = g_ref[...]

    for turn in range(2):
        for k in range(4):
            gt[turn, k] = g_ref[:, tile(place(k, turn), PIECE)].T
    a_slot = ids(16)
    mine = tile(p, ROWS)
    z_in = [send(gt.at[1], zbuf.at[0], (beside, c), a_slot + 3)]
    z_in.append(send(gt.at[1], zbuf.at[1], (beside, far), a_slot + 7))
    a_near = [
        send(gt.at[0, k], at.at[c, :, mine], across(k), a_slot + k - 1) for k in range(1, 4)
    ]
    at[c, :, mine] = gt[0, 0]
    a_cross = []
    far_part(1)

    seen = set()

    def mix(n, j):
        h = order[n]
        if n not in seen:
            seen.add(n)
            wcopies[n].wait()
        if n >= 2:
            j = (p // 2 + j) % 4
        deep = pl.ds(pl.multiple_of(h * DPART + j * DEPTH, DEPTH), DEPTH)
        cols = tile(j, DEPTH)
        gm[...] += jnp.dot(gall[h, :, cols], wv[deep, :], preferred_element_type=F32)

    gm[...] = jnp.zeros_like(gm)
    loads["res"].wait()
    for i in range(TILES):
        lanes = slice(128 * i, 128 * (i + 1))
        rl[pl.ds(i, MODES, stride=8), :] = res_ref[:, lanes] * jnp.sqrt(rate_ref[:, lanes])
    for j in range(4):
        mix(0, j)

    rate = rate_ref[:, tile(p, 128)]
    step_w = jnp.exp(-float(ROWS) * rate)
    layer_w = jnp.exp(-float(ROWS * PLANE) * rate)
    blank = jnp.zeros((MODES, 128), F32)
    arrive(h_in)
    state = blank
    for b in range(PLANE):
        so[b * 16 : (b + 1) * 16, :] = state
        state = step_w * state + hin[b * 16 : (b + 1) * 16, :]
    yin[tile(y, 16), :] = state
    y_in = to_layers(yin, 16)
    g_sib.wait_recv()
    for j in range(4):
        mix(1, j)
    arrive(y_in)
    before = blank
    for b in range(LAYERS):
        before = jnp.where(b < y, layer_w * before + yin[b * 16 : (b + 1) * 16, :], before)
    for b in range(PLANE):
        so[b * 16 : (b + 1) * 16, :] += before
        before = step_w * before
    s_in = to_owners(so, sin, 16)
    far_part(2)
    far_part(3)
    beyond = tile(place(0, 1), ROWS)
    for n, (h, found) in enumerate(((c, a_near), (far, a_cross))):
        z_in[n].wait_recv()
        at[h, :, beyond] = zbuf[n, 0]
        found += [
            send(zbuf.at[n, k], at.at[h, :, beyond], across(k), a_slot + 3 + 4 * n + k)
            for k in range(1, 4)
        ]
    far_pass(1)

    loads["q"].wait()
    arrive(s_in)

    def forward(t, h):
        for u in range(2):
            at_row = t * 2 + u
            x = xs[rows8(at_row), :]
            h = tuple(decay(m) * h[m] + x for m in range(MODES))
            for m in range(MODES):
                hb[rows8(at_row * MODES + m), :] = h[m]
            ys[rows8(at_row), :] = tree([amplitude(m) * h[m] for m in range(MODES)])
        return h

    lax.fori_loop(
        0, ROWS // 2, forward,
        tuple(sin[pl.ds(m, TILES, stride=MODES), :] for m in range(MODES)),
    )

    gat_slot = ids(CHUNKS * (PLANE - 1))
    other = place(0, 1)
    theirs = tile(other, ROWS)
    distant = tile(place(2, 0), ROWS)
    gat_z, gat_x2, gat_in = [], [], []

    def spread(group):
        for chunk in GROUPS[group]:
            spread_one(chunk)

    def spread_one(chunk):
        slot = gat_slot + chunk * (PLANE - 1)
        block = gat[chunk].at[mine]
        gat_z.append(send(block, block, (y * PLANE + other, c), slot))
        gat_x2.append(send(block, block, across(2), slot + 2))
        gat_in.append([send(block, block, across(k), slot + k) for k in (1, 3)])

    def spread_more(group):
        for chunk in GROUPS[group]:
            spread_more_one(chunk)

    def spread_more_one(chunk):
        slot = gat_slot + chunk * (PLANE - 1) + 4
        block = gat[chunk].at[theirs]
        gat_z[chunk].wait_recv()
        gat_in[chunk] += [send(block, block, across(k), slot + k // 2) for k in (1, 3)]
        if chunk in straight:
            gat_in[chunk] += [gat_x2[chunk], send(block, block, across(2), slot + 2)]
            return
        block = gat[chunk].at[distant]
        gat_x2[chunk].wait_recv()
        gat_in[chunk].append(send(block, block, (y * PLANE + other, c), slot + 2))

    straight = GROUPS[0]
    starts = [sum(WIDTHS[:n]) for n in range(CHUNKS)]
    for i in range(TILES):
        lanes = slice(128 * i, 128 * (i + 1))
        out = ys[pl.ds(i, ROWS, stride=8), :].astype(BF16)
        co[:, lanes] = out
        gated = (q_ref[:, lanes].astype(F32) * out.astype(F32)).astype(BF16)
        chunk = max(n for n in range(CHUNKS) if starts[n] <= 128 * i)
        from_lane = 128 * i - starts[chunk]
        gat[chunk][mine, from_lane : from_lane + 128] = gated
        if 128 * (i + 1) == sum(WIDTHS[n] for n in GROUPS[0]):
            spread(0)

    far_part(0)
    far_pass(2)
    g_pass[1].wait_recv()
    mix(3, 1)
    far_pass(3)
    spread(1)
    g_pass[2].wait_recv()
    mix(3, 2)
    arrive(a_near)
    a_sib = [send(at.at[c], at.at[c], (s, sib), a_slot + 14)]
    spread_more(0)
    g_pass[3].wait_recv()
    mix(3, 3)
    far_pass(0)
    arrive(a_cross)
    a_sib.append(send(at.at[far], at.at[far], (s, sib), a_slot + 15))
    g_pass[0].wait_recv()
    mix(3, 0)
    for i in range(TILES):
        lanes = slice(128 * i, 128 * (i + 1))
        mixed = gm[:, lanes].astype(BF16).astype(F32)
        gq_ref[:, lanes] = (mixed * co[:, lanes].astype(F32)).astype(BF16)
        cot = (mixed * q_ref[:, lanes].astype(F32)).astype(BF16)
        cs[pl.ds(i, ROWS, stride=8), :] = cot.astype(F32)

    def behind(n, g):
        for u in range(4):
            cot = cs[rows8(ROWS - 1 - (n * 4 + u)), :]
            g = tuple(decay(m) * g[m] + cot for m in range(MODES))
        return g

    g = lax.fori_loop(0, ROWS // 4, behind, (zero,) * MODES)
    for m in range(MODES):
        gs[pl.ds(m, TILES, stride=MODES), :] = g[m]
    g_in = to_owners(gs, gin, 16)
    spread(2)
    spread_more(1)
    spread(3)
    spread(4)

    half = MODES // 2
    for part in range(2):
        modes = range(part * half, (part + 1) * half)

        def backward(n, carry, modes=modes):
            g, plain, ramp = carry
            for u in range(2):
                at_row = ROWS - 1 - (n * 2 + u)
                cot = cs[rows8(at_row), :]
                states = [hb[rows8(at_row * MODES + m), :] for m in modes]
                g = tuple(decay(m) * g[j] + cot for j, m in enumerate(modes))
                plain = tuple(plain[j] + states[j] * cot for j in range(half))
                ramp = tuple(ramp[j] + states[j] * g[j] for j in range(half))
            return g, plain, ramp

        found = lax.fori_loop(0, ROWS // 2, backward, ((zero,) * half,) * 3)
        for j, m in enumerate(modes):
            for n in range(2):
                pq[pl.ds(n * 16 + m, TILES, stride=48), :] = found[n + 1][j]

    rs_slot = ids(CHUNKS * 3)
    relay_slot = ids(RELAYED * 2)
    rs_in, relay_in = [], []
    top, low = pl.ds(0, PIECE // 2), pl.ds(PIECE // 2, PIECE // 2)

    def partial(chunk, k):
        return jnp.dot(at[(y + k) % LAYERS], gat[chunk][...], preferred_element_type=F32)

    def product(group):
        for chunk in GROUPS[group]:
            product_one(chunk)

    def product_one(chunk):
        arrive(gat_in[chunk])
        slot = rs_slot + chunk * 3
        value = partial(chunk, 2).astype(BF16)
        if chunk < RELAYED:
            relay_send[chunk][...] = value
            relay_in.append([
                send(relay_send[chunk].at[rows], relay_recv[chunk].at[rows], layer(k),
                     relay_slot + chunk * 2 + n)
                for n, (rows, k) in enumerate(((top, 1), (low, 3)))
            ])
            for n, k in enumerate((1, 3)):
                held[chunk][n] = partial(chunk, k)
        else:
            for n, k in ((2, 2), (0, 1), (1, 3)):
                rs_send[chunk][n] = value if k == 2 else partial(chunk, k).astype(BF16)
                rs_in.append(
                    send(rs_send[chunk].at[n], rs_recv[chunk].at[n], layer(k), slot + n)
                )
        own[:, starts[chunk] : starts[chunk] + WIDTHS[chunk]] = partial(chunk, 0)

    def pass_on(group):
        for chunk in GROUPS[group]:
            pass_on_one(chunk)

    def pass_on_one(chunk):
        arrive(relay_in[chunk])
        for n, (k, added, alone) in enumerate(((1, top, low), (3, low, top))):
            value = held[chunk][n, added, :] + relay_recv[chunk][added, :].astype(F32)
            rs_send[chunk][n, added, :] = value.astype(BF16)
            rs_send[chunk][n, alone, :] = held[chunk][n, alone, :].astype(BF16)
            rs_in.append(
                send(rs_send[chunk].at[n], rs_recv[chunk].at[n], layer(k), rs_slot + chunk * 3 + n)
            )

    spread_more(2)
    arrive(a_sib)
    product(0)
    spread_more(3)

    arrive(g_in)
    state = blank
    for b in reversed(range(PLANE)):
        to[b * 16 : b * 16 + 16, :] = state
        state = step_w * state + gin[b * 16 : b * 16 + 16, :]
    yin2[tile(y, 16), :] = state
    y2_in = to_layers(yin2, 16)

    def reach(t, z):
        for u in range(2):
            z = tuple(
                decay(m) * (z[m] + hb[rows8((t * 2 + u) * MODES + m), :]) for m in range(MODES)
            )
        return z

    z = lax.fori_loop(0, ROWS // 2, reach, (zero,) * MODES)
    for m in range(MODES):
        pq[pl.ds(32 + m, TILES, stride=48), :] = z[m]

    pass_on(0)
    product(1)
    spread_more(4)

    arrive(y2_in)
    after, chosen = blank, blank
    for b in reversed(range(LAYERS)):
        chosen = jnp.where(b == y, after, chosen)
        after = layer_w * after + yin2[b * 16 : b * 16 + 16, :]
    for b in reversed(range(PLANE)):
        to[b * 16 : b * 16 + 16, :] += chosen
        chosen = step_w * chosen
    t_in = to_owners(to, tin, 16)
    p_in = to_owners(pq, pin, 48)
    pass_on(1)
    product(2)

    arrive(p_in)
    plain, ramp = blank, blank
    for b in range(PLANE):
        p_b, q_b, z_b = (pin[b * 48 + n * 16 : b * 48 + (n + 1) * 16, :] for n in range(3))
        plain = plain + p_b
        ramp = ramp + q_b + to[b * 16 : b * 16 + 16, :] * z_b
    yp[pl.ds(pl.multiple_of(y * 32, 16), 16), :] = plain
    yp[pl.ds(pl.multiple_of(y * 32 + 16, 16), 16), :] = ramp
    yp_in = to_layers(yp, 32)

    arrive(t_in)

    def final(n, g):
        for u in range(2):
            at_row = ROWS - 1 - (n * 2 + u)
            cot = cs[rows8(at_row), :]
            g = tuple(decay(m) * g[m] + cot for m in range(MODES))
            ys[rows8(at_row), :] = tree([amplitude(m) * g[m] for m in range(MODES)])
        return g

    lax.fori_loop(
        0, ROWS // 2, final,
        tuple(tin[pl.ds(m, TILES, stride=MODES), :] for m in range(MODES)),
    )
    for i in range(TILES):
        lanes = slice(128 * i, 128 * (i + 1))
        back = ys[pl.ds(i, ROWS, stride=8), :].astype(BF16).astype(F32)
        gk_ref[:, lanes] = (back * v_ref[:, lanes].astype(F32)).astype(BF16)
        gv_ref[:, lanes] = (back * k_ref[:, lanes].astype(F32)).astype(BF16)

    pass_on(2)
    product(3)
    product(4)

    arrive(yp_in)
    plain, ramp = blank, blank
    for b in range(LAYERS):
        plain = plain + yp[b * 32 : b * 32 + 16, :]
        ramp = ramp + yp[b * 32 + 16 : b * 32 + 32, :]
    root = jnp.sqrt(rate) * grad_scale
    pr[0:16, :] = root * plain
    pr[16:32, :] = res_ref[:, tile(p, 128)] * root * (0.5 * plain - rate * (ramp - plain))
    slot = ids(PLANE - 1)
    pr_in = [send(pr, prin.at[tile(p, 32)], plane(k), slot + k - 1) for k in range(1, PLANE)]
    prin[tile(p, 32), :] = pr[...]

    arrive(pr_in)
    for i in range(TILES):
        lanes = slice(128 * i, 128 * (i + 1))
        gr_ref[:, lanes] = prin[i * 32 : i * 32 + 16, :]
        gl_ref[:, lanes] = prin[i * 32 + 16 : i * 32 + 32, :]
    arrive(rs_in)
    for chunk in range(CHUNKS):
        cols = slice(starts[chunk], starts[chunk] + WIDTHS[chunk])
        total = own[:, cols]
        for k in range(2 if chunk < RELAYED else 3):
            total = total + rs_recv[chunk][k].astype(F32)
        gw_ref[:, cols] = total * grad_scale
    for copy in sends:
        copy.wait_send()


SLOTS = 192


def settle(*refs):
    count = len(refs) // 2
    for n in range(count):
        refs[count + n][...] = refs[n][...]


def per_device(query_act, key_act, value_act, residue, decay_rate, out_weight, grad_out):
    vmem = pl.BlockSpec(memory_space=pltpu.VMEM)
    shape = jax.ShapeDtypeStruct
    small = shape((ROWS, COLS), BF16)
    modal = shape((MODES, COLS), F32)
    scratch = [
        ((ROWS, COLS), BF16),
        ((ROWS, COLS), BF16),
        ((ROWS, COLS), BF16),
        ((ROWS, DPART), BF16),
        ((MODES, COLS), F32),
        ((MODES, COLS), F32),
        ((PARTS * DPART, COLS), BF16),
        ((ROWS * 8, 128), F32),
        ((ROWS * 8, 128), F32),
        ((ROWS * 8, 128), F32),
        ((ROWS * MODES * 8, 128), F32),
        ((MODES * 8, 128), F32),
        ((MODES * 8, 128), F32),
        ((PARTS, ROWS, DPART), BF16),
        ((2, 4, PIECE, ROWS), BF16),
        ((2, 4, PIECE, ROWS), BF16),
        ((4, PIECE, ROWS), BF16),
        ((PARTS, PIECE, PLANE * ROWS), BF16),
        [((PLANE * ROWS, wide), BF16) for wide in WIDTHS],
        ((ROWS, COLS), F32),
        ((ROWS, COLS), BF16),
        ((TILES * 16, 128), F32),
        ((PLANE * 16, 128), F32),
        ((PLANE * 16, 128), F32),
        ((TILES * 16, 128), F32),
        ((LAYERS * 16, 128), F32),
        ((TILES * 16, 128), F32),
        ((PLANE * 16, 128), F32),
        ((LAYERS * 16, 128), F32),
        ((PLANE * 16, 128), F32),
        ((TILES * 16, 128), F32),
        ((TILES * 48, 128), F32),
        ((PLANE * 48, 128), F32),
        ((LAYERS * 32, 128), F32),
        ((32, 128), F32),
        ((TILES * 32, 128), F32),
        [((3, PIECE, wide), BF16) for wide in WIDTHS],
        [((3, PIECE, wide), BF16) for wide in WIDTHS],
        [((PIECE, wide), BF16) for wide in WIDTHS[:RELAYED]],
        [((PIECE, wide), BF16) for wide in WIDTHS[:RELAYED]],
        [((2, PIECE, wide), F32) for wide in WIDTHS[:RELAYED]],
        ((PIECE, COLS), F32),
    ]
    outs = (small, small, small, shape((PIECE, COLS), F32), modal, modal)
    found = pl.pallas_call(
        body,
        out_shape=outs,
        in_specs=[pl.BlockSpec(memory_space=pl.ANY)] * 7,
        out_specs=(vmem,) * 6,
        scratch_shapes=[
            [pltpu.VMEM(*one) for one in entry] if isinstance(entry, list) else pltpu.VMEM(*entry)
            for entry in scratch
        ]
        + [
            pltpu.SemaphoreType.DMA((10,)),
            pltpu.SemaphoreType.DMA((SLOTS,)),
            pltpu.SemaphoreType.DMA((SLOTS,)),
        ],
        compiler_params=pltpu.CompilerParams(
            collective_id=0, has_side_effects=True, vmem_limit_bytes=56 * 2**20
        ),
        cost_estimate=pl.CostEstimate(
            flops=2 * 2**31, bytes_accessed=20 * 2**20, transcendentals=0
        ),
    )(query_act, key_act, value_act, grad_out, residue, decay_rate, out_weight)
    return pl.pallas_call(
        settle,
        out_shape=outs,
        in_specs=[vmem] * len(outs),
        out_specs=(vmem,) * len(outs),
    )(*found)


def solution(mesh):
    both = P("seq", "chan")
    chan = P(None, "chan")
    return jax.shard_map(
        per_device,
        mesh=mesh,
        in_specs=(both, both, both, chan, chan, chan, both),
        out_specs=(both, both, both, both, chan, chan),
        check_vma=False,
    )
```
